32 devices in a mesh: dp: 8 (over z, y), mp: 4 (over x, core).
Axes of the slice: x: 2, y: 2, z: 4, core: 2. Of those that a mesh axis runs over, the one named last changes fastest.
Arguments:
- tokens: bfloat16 [32768, 512], P(('dp', 'mp')), may hold values from -6 to 6
- sentence_ids: int32 [32768], P(('dp', 'mp')), may hold values from 0 to 2047, as said below
- validity: int32 [32768], P(('dp', 'mp')), may hold values from 0 to 1, as said below
- expert_ids: int32 [32768, 2], P(('dp', 'mp')), may hold values from 0 to 7, all different within a row
- cotangent: bfloat16 [32768, 512], P(('dp', 'mp')), may hold values from -6 to 6
- first_gain: bfloat16 [512], replicated, may hold values from 0.5 to 1.5
- first_shift: bfloat16 [512], replicated, may hold values from -1.5 to 1.5
- router: bfloat16 [512, 8], replicated, may hold values from -0.25 to 0.25
- query_weight: bfloat16 [512, 512], replicated, may hold values from -0.25 to 0.25
- output_weight: bfloat16 [512, 512], replicated, may hold values from -6 to 6
- keyval_weight: bfloat16 [512, 128], replicated, may hold values from -0.25 to 0.25
- second_gain: bfloat16 [512], replicated, may hold values from 0.5 to 1.5
- second_shift: bfloat16 [512], replicated, may hold values from -1.5 to 1.5
- expand_weight: bfloat16 [512, 2048], P(None, 'mp'), may hold values from -0.25 to 0.25
- expand_bias: bfloat16 [2048], P('mp'), may hold values from -1.5 to 1.5
- contract_weight: bfloat16 [2048, 512], P('mp'), may hold values from -0.125 to 0.125
- contract_bias: bfloat16 [512], replicated, may hold values from -1.5 to 1.5
Outputs:
- layer_output: bfloat16 [32768, 512], P(('dp', 'mp'))
- tokens_gradient: bfloat16 [32768, 512], P(('dp', 'mp'))
- first_gain_grad: float32 [512], replicated
- first_shift_grad: float32 [512], replicated
- router_grad: float32 [512, 8], replicated
- query_grad: float32 [512, 512], replicated
- output_grad: float32 [512, 512], replicated
- keyval_grad: float32 [512, 128], replicated
- second_gain_grad: float32 [512], replicated
- second_shift_grad: float32 [512], replicated
- expand_grad: float32 [512, 2048], P(None, 'mp')
- expand_bias_grad: float32 [2048], P('mp')
- contract_grad: float32 [2048, 512], P('mp')
- contract_bias_grad: float32 [512], replicated
The draws below stay inside these ranges and needn't reach their ends.
Inputs may be any that keep to these rules, and one draw needn't show every extreme that they name: `sentence_ids`: each aligned block of 1024 rows holds whole sentences one after another, each with its own id, of 16 to 128 tokens (where a block has no padding its last sentence may be shorter), followed by padding; a padding token's id is 1024 plus its place in the block and equals no other id of the block. Ids are compared only within a block. `validity`: 1 on the sentences' tokens, 0 on padding; in every draw some block of 1024 rows is all 1. `expert_ids`: each token names 2 different experts.
All inputs are finite; a program needn't handle non-finite values.
Results may differ from the reference program's by a relative error of at most 0.015.
Values may be sent and summed in bfloat16 or wider, within the bound.
No kernel may reach another device: no remote copies, remote signals or barrier semaphores. Data moves between devices by JAX's collectives and lax.ppermute only.
A program may use at most 192 MiB of HBM per device.

```python
import jax
import jax.numpy as jnp
from jax import lax

D = 512
FF = 2048
EXPERTS = 8
HEAD = 64
TOP = 2
SENT_MAX = 128
SENT_MIN = 16
TOK_DEV = 1024
TOKENS = 32768


def packing(key):
    slot_count = TOKENS // TOK_DEV
    sentence_count = TOK_DEV // SENT_MIN
    key_len, key_cap, key_full = jax.random.split(jax.random.fold_in(key, 7), 3)
    lengths = jax.random.randint(key_len, (slot_count, sentence_count), SENT_MIN, SENT_MAX + 1)
    ends = jnp.cumsum(lengths, axis=1)
    caps = jax.random.randint(key_cap, (slot_count,), TOK_DEV // 2, TOK_DEV + 1)
    full_slot = jax.random.randint(key_full, (), 0, slot_count)
    slot_index = jnp.arange(slot_count)
    caps = jnp.where(slot_index == full_slot, TOK_DEV, caps)
    kept = ends <= caps[:, None]
    last_end = jnp.max(jnp.where(kept, ends, 0), axis=1)
    position = jnp.arange(TOK_DEV)
    before = jnp.sum((kept[:, :, None] & (ends[:, :, None] <= position[None, None, :])).astype(jnp.int32), axis=1)
    valid = (position[None, :] < last_end[:, None]) | (slot_index[:, None] == full_slot)
    idents = jnp.where(valid, before, TOK_DEV + position[None, :])
    return (idents.reshape(-1).astype(jnp.int32), valid.reshape(-1).astype(jnp.int32))


def draw_sentence_ids(key, part):
    return packing(key)[0]


def draw_validity(key, part):
    return packing(key)[1]


def shard_levels(rng, extent, pieces, smallest, largest):
    factor_of, own = 1.0, jax.random.fold_in(rng, 6)
    for axis_at, parts in pieces:
        heights = jnp.exp(jax.random.uniform(jax.random.fold_in(own, axis_at), (parts,), jnp.float32, smallest / len(pieces), largest / len(pieces)))
        factor_of = factor_of * jnp.repeat(heights, extent[axis_at] // parts).reshape([-1 if axis == axis_at else 1 for axis in range(len(extent))])
    return factor_of


def picks_of(stream_key, rows, amount, top, lift):
    sequence = jax.random.permutation(jax.random.fold_in(stream_key, 1), amount)
    pull = sequence
    for power in range(3):
        pull = pull * pull // amount
    pull = pull * lift // amount
    tickets = jax.random.randint(jax.random.fold_in(stream_key, 2), (rows, amount), 0, 4096) + pull
    sure = jax.random.permutation(jax.random.fold_in(stream_key, 3), rows)[jnp.arange(amount) % rows]
    tickets = jnp.where(jnp.arange(rows)[:, None] == sure[None, :], 1 << 14, tickets)
    merit = tickets * amount + jnp.arange(amount)
    return lax.top_k(merit.astype(jnp.int32), top)[1].astype(jnp.int32)


def gaussian(stream_key, shape, scale, bound, cuts=(), kind=jnp.bfloat16):
    level = shard_levels(stream_key, shape, cuts, -0.22, 0.18) if cuts else 1.0
    drawn = jax.random.normal(stream_key, shape, jnp.float32) * scale * level
    return jnp.minimum(jnp.maximum(drawn, -bound), bound).astype(kind)


def setup_inputs(seed: int = 0) -> dict:
    arg_keys = jax.random.split(jax.random.key(seed), 18)
    return {
        "tokens": gaussian(arg_keys[0], (TOKENS, D), 1.0, 6.0, ((0, 32),)),
        "sentence_ids": draw_sentence_ids(jax.random.fold_in(arg_keys[17], 71), 0),
        "validity": draw_validity(jax.random.fold_in(arg_keys[17], 71), 0),
        "expert_ids": picks_of(arg_keys[3], TOKENS, EXPERTS, TOP, 2048),
        "cotangent": gaussian(arg_keys[4], (TOKENS, D), 1.0, 6.0, ((0, 32),)),
        "first_gain": jnp.clip(1.0 + 0.1 * jax.random.normal(arg_keys[5], (D,), jnp.float32), 0.5, 1.5).astype(jnp.bfloat16),
        "first_shift": gaussian(arg_keys[6], (D,), 0.3, 1.5),
        "router": gaussian(arg_keys[7], (D, EXPERTS), D ** -0.5, 0.25),
        "query_weight": gaussian(arg_keys[8], (D, EXPERTS * HEAD), D ** -0.5, 0.25),
        "output_weight": gaussian(arg_keys[9], (EXPERTS * HEAD, D), 1.0, 6.0),
        "keyval_weight": gaussian(arg_keys[10], (D, 2 * HEAD), D ** -0.5, 0.25),
        "second_gain": jnp.clip(1.0 + 0.1 * jax.random.normal(arg_keys[11], (D,), jnp.float32), 0.5, 1.5).astype(jnp.bfloat16),
        "second_shift": gaussian(arg_keys[12], (D,), 0.3, 1.5),
        "expand_weight": gaussian(arg_keys[13], (D, FF), D ** -0.5, 0.25, ((1, 4),)),
        "expand_bias": gaussian(arg_keys[14], (FF,), 0.3, 1.5, ((0, 4),)),
        "contract_weight": gaussian(arg_keys[15], (FF, D), FF ** -0.5, 0.125, ((0, 4),)),
        "contract_bias": gaussian(arg_keys[16], (D,), 0.3, 1.5),
    }


@jax.custom_vjp
def low(v):
    return lax.optimization_barrier(v.astype(jnp.bfloat16)).astype(jnp.float32)

@jax.custom_vjp
def low_back(v):
    return v

def low_keep(v):
    return (low(v), None)

def low_pass(kept, grad):
    return (grad,)

def back_keep(v):
    return (v, None)

def back_low(kept, grad):
    return (low(grad),)
low.defvjp(low_keep, low_pass)
low_back.defvjp(back_keep, back_low)
epsilon = 1e-05

def normalize(rows_in, gain, shift):
    middle = lax.optimization_barrier(jnp.mean(rows_in, axis=-1, keepdims=True))
    center = rows_in - middle
    spread = lax.optimization_barrier(jnp.mean(center * center, axis=-1, keepdims=True))
    return center * lax.rsqrt(spread + epsilon) * gain + shift

def product(left, right):
    return jnp.dot(left, right, precision=lax.Precision.HIGHEST, preferred_element_type=jnp.float32)

def attend_slot(operands):
    query_slot, key_slot, value_slot, ident_slot = operands
    raw_scores = low_back(jnp.einsum('qeh,kh->eqk', query_slot, key_slot, precision=lax.Precision.HIGHEST))
    same = ident_slot[:, None] == ident_slot[None, :]
    scores = jnp.where(same[None], raw_scores * HEAD ** (-0.5), -1e+30)
    chances = low(jax.nn.softmax(scores, axis=-1))
    return low_back(jnp.einsum('eqk,kh->qeh', chances, value_slot, precision=lax.Precision.HIGHEST))

def reference(tokens, sentence_ids, validity, expert_ids, cotangent, first_gain, first_shift, router, query_weight, output_weight, keyval_weight, second_gain, second_shift, expand_weight, expand_bias, contract_weight, contract_bias):
    slot_count = TOKENS // TOK_DEV
    chosen = (expert_ids[:, :, None] == jnp.arange(EXPERTS, dtype=jnp.int32)[None, None, :]).astype(jnp.float32)
    idents = sentence_ids.reshape(slot_count, TOK_DEV)

    def forward(inputs, gain_one, shift_one, route_w, query_w, out_w, keyval_w, gain_two, shift_two, expand_w, expand_b, contract_w, contract_b):
        first_normed = low(normalize(inputs, gain_one, shift_one))
        logits = low_back(product(first_normed, route_w))
        picked = lax.optimization_barrier(jnp.sum(chosen * logits[:, None, :], axis=-1))
        paired = jax.nn.softmax(picked, axis=-1)
        gating = lax.optimization_barrier(jnp.sum(paired[:, :, None] * chosen, axis=1))
        queries = low_back(low(product(first_normed, query_w)))
        keyval = low_back(low(product(first_normed, keyval_w)))
        context = lax.map(jax.checkpoint(attend_slot), (queries.reshape(slot_count, TOK_DEV, EXPERTS, HEAD), keyval[:, :HEAD].reshape(slot_count, TOK_DEV, HEAD), keyval[:, HEAD:].reshape(slot_count, TOK_DEV, HEAD), idents))
        context = context.reshape(TOKENS, EXPERTS * HEAD)
        mixed = low(context * jnp.repeat(gating, HEAD, axis=1))
        residual = inputs + low_back(product(mixed, out_w))
        second_normed = low(normalize(residual, gain_two, shift_two))
        hidden = low(jax.nn.gelu(low_back(product(second_normed, expand_w) + expand_b), approximate=False))
        return residual + low_back(product(hidden, contract_w)) + contract_b
    params = tuple((item.astype(jnp.float32) for item in (tokens, first_gain, first_shift, router, query_weight, output_weight, keyval_weight, second_gain, second_shift, expand_weight, expand_bias, contract_weight, contract_bias)))
    result, pullback = jax.vjp(forward, *params)
    grad_out = cotangent.astype(jnp.float32) * validity.astype(jnp.float32)[:, None]
    grads = pullback(grad_out)
    return (result.astype(jnp.bfloat16), grads[0].astype(jnp.bfloat16), grads[1], grads[2], grads[3], grads[4], grads[5], grads[6], grads[7], grads[8], grads[9], grads[10], grads[11], grads[12])
```

```python
import functools
import math

import jax
import jax.numpy as jnp
from jax import lax
from jax.experimental import pallas as pl
from jax.experimental.pallas import tpu as pltpu
from jax.sharding import PartitionSpec as P

F32 = jnp.float32
BF16 = jnp.bfloat16
epsilon = 1e-05
AXES = ("dp", "mp")
TILE = 128
VMEM_LIMIT = 56 << 20
LANES = 128
VECTOR_ROW = 8


def dot(left, right):
    return lax.dot_general(left, right, (((1,), (0,)), ((), ())), preferred_element_type=F32)


def dot_nt(left, right):
    return lax.dot_general(left, right, (((1,), (1,)), ((), ())), preferred_element_type=F32)


def dot_tn(left, right):
    return lax.dot_general(left, right, (((0,), (0,)), ((), ())), preferred_element_type=F32)


def normed(rows_in):
    middle = jnp.mean(rows_in, axis=-1, keepdims=True)
    center = rows_in - middle
    inverse = lax.rsqrt(jnp.mean(center * center, axis=-1, keepdims=True) + epsilon)
    return center * inverse, inverse


def norm_back(grad_normed, gain, normed_hat, inverse):
    scaled = grad_normed * gain
    mean_one = jnp.mean(scaled, axis=-1, keepdims=True)
    mean_two = jnp.mean(scaled * normed_hat, axis=-1, keepdims=True)
    return inverse * (scaled - mean_one - normed_hat * mean_two)


def row_sum(values):
    return jnp.sum(values, axis=0, keepdims=True)


def pair_masks(first_id, second_id, pairs):
    half = (lax.broadcasted_iota(jnp.int32, (TILE, LANES), 1) >= LANES // 2).astype(F32)
    low = first_id - half
    high = second_id - half
    return [(low == 2.0 * pair, high == 2.0 * pair) for pair in range(pairs)]


def window_of(tile, tiles):
    width = min(3, tiles)
    return min(max(tile - 1, 0), tiles - width) * TILE, width * TILE


def attend_kernel(
    tok, sent, valid, expert, cot, gain1, shift1, router, wq, wkv, wo, gain2, shift2,
    res, low2, glow, low1, mixed, qsel, kv, chance, ctx, cols,
    queries, logits,
):
    rows, width = tok.shape
    tiles = rows // TILE
    pairs = width // LANES
    big = 256
    scale = (wkv.shape[1] // 2) ** -0.5
    half_lane = lax.broadcasted_iota(jnp.int32, (big, LANES), 1) < LANES // 2
    for at in range(0, rows, big):
        span = pl.ds(at, big)
        hat, _ = normed(tok[span, :].astype(F32))
        low = (hat * gain1[...].astype(F32) + shift1[...].astype(F32)).astype(BF16)
        low1[span, :] = low
        queries[span, :] = dot(low, wq[...]).astype(BF16)
        logits[span, :] = dot(low, router[...])
        both = dot(low, wkv[...])
        turned = pltpu.roll(both, LANES // 2, 1)
        kv[span, :LANES] = jnp.where(half_lane, both, turned).astype(BF16)
        kv[span, LANES:] = jnp.where(half_lane, turned, both).astype(BF16)
    for tile in range(tiles):
        at = tile * TILE
        span = pl.ds(at, TILE)
        meta = jnp.concatenate(
            [
                sent[:, at : at + TILE],
                valid[:, at : at + TILE],
                expert[:, at : at + TILE],
                jnp.zeros((4, TILE), jnp.int32),
            ],
            axis=0,
        ).astype(F32)
        column = jnp.transpose(meta)
        own_sent, own_valid = column[:, 0:1], column[:, 1:2]
        first_id, second_id = column[:, 2:3], column[:, 3:4]
        glow[span, :] = jnp.where(own_valid > 0.5, cot[span, :].astype(F32), 0.0).astype(BF16)
        scored = logits[span, :]
        slot = lax.broadcasted_iota(jnp.int32, scored.shape, 1).astype(F32)
        pick0 = jnp.sum(jnp.where(slot == first_id, scored, 0.0), axis=-1, keepdims=True)
        pick1 = jnp.sum(jnp.where(slot == second_id, scored, 0.0), axis=-1, keepdims=True)
        most = jnp.maximum(pick0, pick1)
        raise0, raise1 = jnp.exp(pick0 - most), jnp.exp(pick1 - most)
        gate0 = raise0 / (raise0 + raise1)
        gate1 = raise1 / (raise0 + raise1)
        lane = lax.broadcasted_iota(jnp.int32, (TILE, 8), 1)
        cols[span, :] = jnp.where(
            lane == 0, gate0, jnp.where(lane == 1, gate1, jnp.where(lane == 2, first_id, second_id))
        )
        masks = pair_masks(first_id, second_id, pairs)
        q0 = jnp.zeros((TILE, LANES), F32)
        q1 = jnp.zeros((TILE, LANES), F32)
        for pair in range(pairs):
            block = queries[span, pair * LANES : (pair + 1) * LANES].astype(F32)
            q0 = jnp.where(masks[pair][0], block, q0)
            q1 = jnp.where(masks[pair][1], block, q1)
        picked = (jnp.concatenate([q0, q1], axis=0) * scale).astype(BF16)
        qsel[tile] = picked
        start, extent = window_of(tile, tiles)
        near = pl.ds(start, extent)
        scores = dot_nt(picked, kv[near, :LANES])
        same = own_sent == sent[:, start : start + extent].astype(F32)
        same = jnp.concatenate([same, same], axis=0)
        scores = jnp.where(same, scores, -1e30)
        weights = jnp.exp(scores - jnp.max(scores, axis=-1, keepdims=True))
        share = (weights * (1.0 / jnp.sum(weights, axis=-1, keepdims=True))).astype(BF16)
        chance[tile] = share
        context = dot(share, kv[near, LANES:])
        ctx[tile] = context
        part0 = context[:TILE] * gate0
        part1 = context[TILE:] * gate1
        for pair in range(pairs):
            mixed[span, pair * LANES : (pair + 1) * LANES] = jnp.where(
                masks[pair][0], part0, jnp.where(masks[pair][1], part1, 0.0)
            ).astype(BF16)
    for at in range(0, rows, big):
        span = pl.ds(at, big)
        total = tok[span, :].astype(F32) + dot(mixed[span, :], wo[...])
        res[span, :] = total
        hat, _ = normed(total)
        low2[span, :] = (hat * gain2[...].astype(F32) + shift2[...].astype(F32)).astype(BF16)


def ffn_kernel(*refs, more, last, steps):
    low2, glow, expand, contract, bias = refs[:5]
    at = 5
    if "rows" in more:
        out_in, second_in = refs[at : at + 2]
        at += 2
    if "weights" in more:
        contract_in, expand_in, bias_in = refs[at : at + 3]
        at += 3
    out, second, contract_out, expand_out, bias_out, contract_sum, expand_sum, bias_sum = refs[at:]
    step = pl.program_id(0)

    @pl.when(step == 0)
    def _():
        if "weights" in more:
            contract_sum[...] = contract_in[...]
            expand_sum[...] = expand_in[...]
            bias_sum[...] = bias_in[...]
        else:
            contract_sum[...] = jnp.zeros_like(contract_sum)
            expand_sum[...] = jnp.zeros_like(expand_sum)
            bias_sum[...] = jnp.zeros_like(bias_sum)

    rows, grads = low2[...], glow[...]
    preact = dot(rows, expand[...]) + bias[...].astype(F32)
    cumulative = 0.5 * (1.0 + lax.erf(preact * (1.0 / math.sqrt(2.0))))
    bell = jnp.exp(-0.5 * preact * preact) * (1.0 / math.sqrt(2.0 * math.pi))
    hidden = (preact * cumulative).astype(BF16)
    grad = (dot_nt(grads, contract[...]) * (cumulative + preact * bell)).astype(BF16)
    bias_sum[...] += row_sum(grad.astype(F32))
    out_part = dot(hidden, contract[...])
    second_part = dot_nt(grad, expand[...])
    if "rows" in more:
        out_part += out_in[...]
        second_part += second_in[...]
    out[...] = out_part.astype(out.dtype)
    second[...] = second_part.astype(second.dtype)
    contract_sum[...] += dot_tn(hidden, grads)
    expand_sum[...] += dot_tn(rows, grad)

    @pl.when(step == steps - 1)
    def _():
        contract_out[...] = contract_sum[...].astype(contract_out.dtype)
        expand_out[...] = expand_sum[...].astype(expand_out.dtype)
        bias_out[...] = bias_sum[...]


def ffn(low2, glow, weights, rows_in=None, weights_in=None, rows_dtype=F32, weights_dtype=F32):
    expand, contract, bias = weights
    rows, width = low2.shape
    units = expand.shape[1]
    step_rows = min(256, rows)
    steps = rows // step_rows
    more = []
    row_spec = pl.BlockSpec((step_rows, width), lambda i: (i, 0))

    def whole(*shape):
        return pl.BlockSpec(shape, lambda i: (0, 0))

    operands = [low2, glow, expand, contract, bias]
    in_specs = [row_spec, row_spec, whole(width, units), whole(units, width), whole(1, units)]
    if rows_in is not None:
        more.append("rows")
        operands += rows_in
        in_specs += [row_spec, row_spec]
    if weights_in is not None:
        more.append("weights")
        operands += weights_in
        in_specs += [whole(units, width), whole(width, units), whole(1, units)]
    outs = pl.pallas_call(
        functools.partial(ffn_kernel, more=tuple(more), last=True, steps=steps),
        grid=(steps,),
        in_specs=in_specs,
        out_specs=[
            row_spec, row_spec, whole(units, width), whole(width, units), whole(1, units)
        ],
        out_shape=[
            jax.ShapeDtypeStruct((rows, width), rows_dtype),
            jax.ShapeDtypeStruct((rows, width), rows_dtype),
            jax.ShapeDtypeStruct((units, width), weights_dtype),
            jax.ShapeDtypeStruct((width, units), weights_dtype),
            jax.ShapeDtypeStruct((1, units), F32),
        ],
        scratch_shapes=[
            pltpu.VMEM((units, width), F32),
            pltpu.VMEM((width, units), F32),
            pltpu.VMEM((1, units), F32),
        ],
        compiler_params=pltpu.CompilerParams(vmem_limit_bytes=VMEM_LIMIT),
        name="ffn",
    )(*operands)
    return list(outs[:2]), list(outs[2:])


def back_kernel(
    out_own, out_got, second_own, second_got, res, tok, glow, low1, mixed, qsel, kv, chance, ctx,
    cols, gain1, gain2, contract_bias, router, wq, wkv, wo, unit_bias,
    layer, tok_grad, packed,
    grad_res, grad_mixed, grad_q, grad_log, key_sum, value_sum, vectors,
):
    rows, width = tok.shape
    tiles = rows // TILE
    pairs = width // LANES
    big = 256
    scale = (wkv.shape[1] // 2) ** -0.5
    experts = router.shape[1]
    gain_one, gain_two = gain1[...].astype(F32), gain2[...].astype(F32)
    gain2_sum = shift2_sum = bias_sum = jnp.zeros((1, width), F32)
    for at in range(0, rows, big):
        span = pl.ds(at, big)
        total = res[span, :]
        layer[span, :] = (
            total + out_own[span, :] + out_got[span, :].astype(F32) + contract_bias[...].astype(F32)
        ).astype(BF16)
        hat, inverse = normed(total)
        second = second_own[span, :] + second_got[span, :].astype(F32)
        gain2_sum += row_sum(second * hat)
        shift2_sum += row_sum(second)
        outer = glow[span, :].astype(F32)
        bias_sum += row_sum(outer)
        grad = outer + norm_back(second, gain_two, hat, inverse)
        grad_res[span, :] = grad
        grad_mixed[span, :] = dot_nt(grad.astype(BF16), wo[...])
    packed[:, width : 2 * width] = dot_tn(mixed[...], grad_res[...].astype(BF16)).astype(BF16)
    key_sum[...] = jnp.zeros_like(key_sum)
    value_sum[...] = jnp.zeros_like(value_sum)
    for tile in range(tiles):
        at = tile * TILE
        span = pl.ds(at, TILE)
        gate0, gate1 = cols[span, 0:1], cols[span, 1:2]
        first_id, second_id = cols[span, 2:3], cols[span, 3:4]
        masks = pair_masks(first_id, second_id, pairs)
        g0 = jnp.zeros((TILE, LANES), F32)
        g1 = jnp.zeros((TILE, LANES), F32)
        for pair in range(pairs):
            block = grad_mixed[span, pair * LANES : (pair + 1) * LANES]
            g0 = jnp.where(masks[pair][0], block, g0)
            g1 = jnp.where(masks[pair][1], block, g1)
        context = ctx[tile]
        use0 = jnp.sum(g0 * context[:TILE], axis=-1, keepdims=True)
        use1 = jnp.sum(g1 * context[TILE:], axis=-1, keepdims=True)
        usual = gate0 * use0 + gate1 * use1
        lane = lax.broadcasted_iota(jnp.int32, (TILE, LANES), 1).astype(F32)
        grad_log[span, :] = jnp.where(
            lane == first_id,
            gate0 * (use0 - usual),
            jnp.where(lane == second_id, gate1 * (use1 - usual), 0.0),
        ).astype(BF16)
        grad_ctx = jnp.concatenate([g0 * gate0, g1 * gate1], axis=0).astype(BF16)
        delta = jnp.sum(grad_ctx.astype(F32) * context, axis=-1, keepdims=True)
        start, extent = window_of(tile, tiles)
        near = pl.ds(start, extent)
        grad_share = dot_nt(grad_ctx, kv[near, LANES:])
        share = chance[tile]
        raw = (share.astype(F32) * (grad_share - delta)).astype(BF16)
        grad_query = dot(raw, kv[near, :LANES]) * scale
        for pair in range(pairs):
            grad_q[span, pair * LANES : (pair + 1) * LANES] = jnp.where(
                masks[pair][0],
                grad_query[:TILE],
                jnp.where(masks[pair][1], grad_query[TILE:], 0.0),
            ).astype(BF16)
        key_sum[near, :] += dot_tn(raw, qsel[tile])
        value_sum[near, :] += dot_tn(share, grad_ctx)
    keys, values = key_sum[...], value_sum[...]
    keys = keys + pltpu.roll(keys, LANES // 2, 1)
    values = values + pltpu.roll(values, LANES // 2, 1)
    half_lane = lax.broadcasted_iota(jnp.int32, (rows, LANES), 1) < LANES // 2
    grad_kv = jnp.where(half_lane, keys, values).astype(BF16)
    gain1_sum = shift1_sum = jnp.zeros((1, width), F32)
    for at in range(0, rows, big):
        span = pl.ds(at, big)
        hat, inverse = normed(tok[span, :].astype(F32))
        grad = (
            dot_nt(grad_q[span, :], wq[...])
            + dot_nt(grad_kv[at : at + big], wkv[...])
            + dot_nt(grad_log[span, :experts], router[...])
        )
        gain1_sum += row_sum(grad * hat)
        shift1_sum += row_sum(grad)
        tok_grad[span, :] = (grad_res[span, :] + norm_back(grad, gain_one, hat, inverse)).astype(
            BF16
        )
    packed[:, :width] = dot_tn(low1[...], grad_q[...]).astype(BF16)
    packed[:, 2 * width : 2 * width + LANES] = dot_tn(low1[...], grad_kv).astype(BF16)
    vectors[...] = jnp.zeros_like(vectors)
    sums = (gain1_sum, shift1_sum, gain2_sum, shift2_sum, bias_sum)
    for place, values in enumerate(sums):
        vectors[VECTOR_ROW + place : VECTOR_ROW + place + 1, :] = values
    first = VECTOR_ROW + len(sums)
    count, units = unit_bias.shape
    vectors[first : first + count, :units] = unit_bias[...]
    packed[:, 2 * width + LANES :] = (
        dot_tn(low1[...], grad_log[...]) + jnp.transpose(vectors[...])
    ).astype(BF16)


def vmem_call(kernel, name, operands, out_shape, scratch):
    return pl.pallas_call(
        kernel,
        out_shape=out_shape,
        in_specs=[pl.BlockSpec(memory_space=pltpu.VMEM)] * len(operands),
        out_specs=[pl.BlockSpec(memory_space=pltpu.VMEM)] * len(out_shape),
        scratch_shapes=scratch,
        compiler_params=pltpu.CompilerParams(vmem_limit_bytes=VMEM_LIMIT),
        name=name,
    )(*operands)


def swap(values, bit, devices):
    return lax.ppermute(values, AXES, [(at, at ^ bit) for at in range(devices)])


def halves(values, mine):
    size = values.shape[0] // 2
    keep = lax.dynamic_slice_in_dim(values, mine * size, size, 0)
    send = lax.dynamic_slice_in_dim(values, (1 - mine) * size, size, 0)
    return keep, send


def scatter_sum(values, bits, place, devices):
    for bit in bits:
        mine = (place // bit) % 2
        keep, send = halves(values, mine)
        got = swap(send, bit, devices)
        values = (keep.astype(F32) + got.astype(F32)).astype(BF16)
    return values


def gather(values, bits, place, devices):
    for bit in reversed(bits):
        mine = (place // bit) % 2
        got = swap(values, bit, devices)
        values = jnp.where(
            mine == 0,
            jnp.concatenate([values, got], axis=0),
            jnp.concatenate([got, values], axis=0),
        )
    return values


def shards(
    n_dp,
    n_mp,
    tokens,
    sentence_ids,
    validity,
    expert_ids,
    cotangent,
    first_gain,
    first_shift,
    router,
    query_weight,
    output_weight,
    keyval_weight,
    second_gain,
    second_shift,
    expand_weight,
    expand_bias,
    contract_weight,
    contract_bias,
):
    devices = n_dp * n_mp
    rows, width = tokens.shape
    units = expand_weight.shape[1]
    tiles = rows // TILE
    _, extent = window_of(0, tiles)
    place = lax.axis_index(AXES)
    mp_place = lax.axis_index("mp")

    def row(vector):
        return vector.reshape(1, -1)

    def shape(*dims, dtype=BF16):
        return jax.ShapeDtypeStruct(dims, dtype)

    bias_row = row(expand_bias)
    own = (expand_weight, contract_weight, bias_row)
    chips = n_mp // 2
    others = [
        tuple(swap(item, 2 * step, devices) for item in own) for step in range(1, chips)
    ]
    operands = [
        tokens, row(sentence_ids), row(validity), expert_ids.T, cotangent, row(first_gain),
        row(first_shift), router, query_weight, keyval_weight, output_weight, row(second_gain),
        row(second_shift),
    ]
    res, low2, glow, low1, mixed, qsel, kv, chance, ctx, cols = vmem_call(
        attend_kernel,
        "attend",
        operands,
        [
            shape(rows, width, dtype=F32),
            shape(rows, width),
            shape(rows, width),
            shape(rows, width),
            shape(rows, width),
            shape(tiles, 2 * TILE, LANES),
            shape(rows, 2 * LANES),
            shape(tiles, 2 * TILE, extent),
            shape(tiles, 2 * TILE, LANES, dtype=F32),
            shape(rows, 8, dtype=F32),
        ],
        [pltpu.VMEM((rows, width), BF16), pltpu.VMEM((rows, router.shape[1]), F32)],
    )
    low2_pair = swap(low2, 1, devices)
    glow_pair = swap(glow, 1, devices)
    rows_own, grads_own = ffn(low2, glow, own)
    rows_pair, grads_own = ffn(
        low2_pair, glow_pair, own, weights_in=grads_own, weights_dtype=BF16
    )
    contract_sum, expand_sum = grads_own[0], grads_own[1]
    unit_rows = jnp.arange(n_mp, dtype=jnp.int32)[:, None]
    unit_bias = jnp.where(unit_rows == mp_place, grads_own[2], 0.0)
    for step in range(1, chips):
        final = step == chips - 1
        rows_pair, grads = ffn(
            low2_pair,
            glow_pair,
            others[step - 1],
            rows_in=rows_pair,
            rows_dtype=BF16 if final else F32,
        )
        if final:
            out_got, second_got = (swap(item, 1, devices) for item in rows_pair)
        rows_own, grads = ffn(
            low2,
            glow,
            others[step - 1],
            rows_in=rows_own,
            weights_in=grads,
            weights_dtype=BF16,
        )
        unit_bias += jnp.where(unit_rows == (mp_place ^ (2 * step)), grads[2], 0.0)
        contract_got = swap(grads[0], 2 * step, devices)
        expand_got = swap(grads[1], 2 * step, devices)
        contract_sum = (contract_sum.astype(F32) + contract_got.astype(F32)).astype(BF16)
        expand_sum = (expand_sum.astype(F32) + expand_got.astype(F32)).astype(BF16)
    layer, tok_grad, packed = vmem_call(
        back_kernel,
        "back",
        [
            rows_own[0], out_got, rows_own[1], second_got, res, tokens, glow, low1, mixed, qsel,
            kv, chance, ctx, cols, row(first_gain), row(second_gain), row(contract_bias), router,
            query_weight, keyval_weight, output_weight, unit_bias,
        ],
        [shape(rows, width), shape(rows, width), shape(width, 2 * width + 2 * LANES)],
        [
            pltpu.VMEM((rows, width), F32),
            pltpu.VMEM((rows, width), F32),
            pltpu.VMEM((rows, width), BF16),
            pltpu.VMEM((rows, LANES), BF16),
            pltpu.VMEM((rows, LANES), F32),
            pltpu.VMEM((rows, LANES), F32),
            pltpu.VMEM((LANES, width), F32),
        ],
    )
    dp_bits = [n_mp << at for at in range(n_dp.bit_length() - 1)]
    turned = dp_bits[1:] + dp_bits[:1]
    mp_bits = [1 << at for at in range(n_mp.bit_length() - 1)]
    contract_grad = gather(
        scatter_sum(contract_sum, dp_bits, place, devices), dp_bits, place, devices
    ).astype(F32)
    expand_grad = gather(
        scatter_sum(expand_sum, turned, place, devices), turned, place, devices
    ).astype(F32)
    every = mp_bits + dp_bits
    packed = gather(scatter_sum(packed, every, place, devices), every, place, devices).astype(F32)
    vectors = packed[:, 2 * width + LANES :].T
    first = VECTOR_ROW + 5
    unit_grad = lax.dynamic_slice_in_dim(vectors, first + mp_place, 1, 0)[0, :units]
    return (
        layer,
        tok_grad,
        vectors[VECTOR_ROW],
        vectors[VECTOR_ROW + 1],
        packed[:, 2 * width + LANES : 2 * width + LANES + router.shape[1]],
        packed[:, :width],
        packed[:, width : 2 * width],
        packed[:, 2 * width : 2 * width + LANES],
        vectors[VECTOR_ROW + 2],
        vectors[VECTOR_ROW + 3],
        expand_grad,
        unit_grad,
        contract_grad,
        vectors[VECTOR_ROW + 4],
    )


def solution(mesh):
    tokens_spec = P(AXES, None)
    placed = (
        tokens_spec,
        P(AXES),
        P(AXES),
        tokens_spec,
        tokens_spec,
        P(),
        P(),
        P(),
        P(),
        P(),
        P(),
        P(),
        P(),
        P(None, "mp"),
        P("mp"),
        P("mp", None),
        P(),
    )
    return jax.shard_map(
        functools.partial(shards, mesh.shape["dp"], mesh.shape["mp"]),
        mesh=mesh,
        in_specs=placed,
        out_specs=(
            tokens_spec,
            tokens_spec,
            P(),
            P(),
            P(),
            P(),
            P(),
            P(),
            P(),
            P(),
            P(None, "mp"),
            P("mp"),
            P("mp", None),
            P(),
        ),
        check_vma=False,
    )
```

```python
import functools
import math

import jax
import jax.numpy as jnp
from jax import lax
from jax.experimental import pallas as pl
from jax.experimental.pallas import tpu as pltpu
from jax.sharding import PartitionSpec as P

F32 = jnp.float32
BF16 = jnp.bfloat16
epsilon = 1e-05
AXES = ("dp", "mp")
TILE = 128
BIG = 256
VMEM_LIMIT = 36 << 20
LANES = 128
VECTOR_ROW = 8


def dot(left, right):
    return lax.dot_general(left, right, (((1,), (0,)), ((), ())), preferred_element_type=F32)


def dot_nt(left, right):
    return lax.dot_general(left, right, (((1,), (1,)), ((), ())), preferred_element_type=F32)


def dot_tn(left, right):
    return lax.dot_general(left, right, (((0,), (0,)), ((), ())), preferred_element_type=F32)


def normed(rows_in):
    middle = jnp.mean(rows_in, axis=-1, keepdims=True)
    center = rows_in - middle
    inverse = lax.rsqrt(jnp.mean(center * center, axis=-1, keepdims=True) + epsilon)
    return center * inverse, inverse


def norm_back(grad_normed, gain, normed_hat, inverse):
    scaled = grad_normed * gain
    mean_one = jnp.mean(scaled, axis=-1, keepdims=True)
    mean_two = jnp.mean(scaled * normed_hat, axis=-1, keepdims=True)
    return inverse * (scaled - mean_one - normed_hat * mean_two)


def as_row(vector):
    return vector[...].astype(F32).reshape(1, -1)


def row_sum(values):
    return jnp.sum(values, axis=0, keepdims=True)


def pair_masks(first_id, second_id, pairs):
    half = (lax.broadcasted_iota(jnp.int32, (TILE, LANES), 1) >= LANES // 2).astype(F32)
    low = first_id - half
    high = second_id - half
    return [(low == 2.0 * pair, high == 2.0 * pair) for pair in range(pairs)]


def window_of(tile, tiles):
    width = min(3, tiles)
    return min(max(tile - 1, 0), tiles - width) * TILE, width * TILE


class Copies:
    def __init__(self, semaphores):
        self.semaphores = semaphores
        self.used = 0
        self.pending = {}

    def start(self, name, source, target):
        copy = pltpu.make_async_copy(source, target, self.semaphores.at[self.used])
        self.used += 1
        copy.start()
        self.pending.setdefault(name, []).append(copy)

    def wait(self, *names):
        for name in names:
            for copy in self.pending.pop(name, ()):
                copy.wait()

    def finish(self):
        self.wait(*list(self.pending))


def attend_kernel(
    sent, valid, expert, gain1, shift1, gain2, shift2, router,
    tok_far, wq_far, wkv_far, cot_far, wo_far,
    res_far, low2_far, glow_far, mixed_far, qsel_far, kv_far, chance_far, gates_far,
    tok, wq, wkv, cot, wo,
    res, low2, glow, mixed, qsel, kv, chance, gates,
    queries, logits, semaphores,
):
    rows, width = tok.shape
    tiles = rows // TILE
    pairs = width // LANES
    scale = (wkv.shape[1] // 2) ** -0.5
    copies = Copies(semaphores)
    copies.start("tok", tok_far, tok)
    copies.start("wq", wq_far, wq)
    copies.start("wkv", wkv_far, wkv)
    copies.start("cot", cot_far, cot)
    copies.start("wo", wo_far, wo)
    half_lane = lax.broadcasted_iota(jnp.int32, (BIG, LANES), 1) < LANES // 2
    copies.wait("tok", "wq", "wkv")
    for at in range(0, rows, BIG):
        span = pl.ds(at, BIG)
        hat, _ = normed(tok[span, :].astype(F32))
        low = (hat * as_row(gain1) + as_row(shift1)).astype(BF16)
        queries[span, :] = dot(low, wq[...]).astype(BF16)
        logits[span, :] = dot_nt(low, router[...])
        both = dot(low, wkv[...])
        turned = pltpu.roll(both, LANES // 2, 1)
        kv[span, :LANES] = jnp.where(half_lane, both, turned).astype(BF16)
        kv[span, LANES:] = jnp.where(half_lane, turned, both).astype(BF16)
    copies.start("out", kv, kv_far)
    copies.wait("cot", "wo")
    for tile in range(tiles):
        at = tile * TILE
        span = pl.ds(at, TILE)
        meta = jnp.concatenate(
            [
                sent[:, at : at + TILE],
                valid[:, at : at + TILE],
                expert[:, at : at + TILE],
                jnp.zeros((4, TILE), jnp.int32),
            ],
            axis=0,
        ).astype(F32)
        column = jnp.transpose(meta)
        own_sent, own_valid = column[:, 0:1], column[:, 1:2]
        first_id, second_id = column[:, 2:3], column[:, 3:4]
        glow[span, :] = jnp.where(own_valid > 0.5, cot[span, :].astype(F32), 0.0).astype(BF16)
        scored = logits[span, :]
        slot = lax.broadcasted_iota(jnp.int32, scored.shape, 1).astype(F32)
        pick0 = jnp.sum(jnp.where(slot == first_id, scored, 0.0), axis=-1, keepdims=True)
        pick1 = jnp.sum(jnp.where(slot == second_id, scored, 0.0), axis=-1, keepdims=True)
        most = jnp.maximum(pick0, pick1)
        raise0, raise1 = jnp.exp(pick0 - most), jnp.exp(pick1 - most)
        gate0 = raise0 / (raise0 + raise1)
        gate1 = raise1 / (raise0 + raise1)
        lane = lax.broadcasted_iota(jnp.int32, (TILE, 8), 1)
        gates[:, at : at + TILE] = jnp.transpose(
            jnp.where(
                lane == 0,
                gate0,
                jnp.where(lane == 1, gate1, jnp.where(lane == 2, first_id, second_id)),
            )
        )
        masks = pair_masks(first_id, second_id, pairs)
        q0 = jnp.zeros((TILE, LANES), F32)
        q1 = jnp.zeros((TILE, LANES), F32)
        for pair in range(pairs):
            block = queries[span, pair * LANES : (pair + 1) * LANES].astype(F32)
            q0 = jnp.where(masks[pair][0], block, q0)
            q1 = jnp.where(masks[pair][1], block, q1)
        picked = (jnp.concatenate([q0, q1], axis=0) * scale).astype(BF16)
        qsel[tile] = picked
        start, extent = window_of(tile, tiles)
        near = pl.ds(start, extent)
        scores = dot_nt(picked, kv[near, :LANES])
        same = own_sent == sent[:, start : start + extent].astype(F32)
        same = jnp.concatenate([same, same], axis=0)
        scores = jnp.where(same, scores, -1e30)
        weights = jnp.exp(scores - jnp.max(scores, axis=-1, keepdims=True))
        share = (weights * (1.0 / jnp.sum(weights, axis=-1, keepdims=True))).astype(BF16)
        chance[tile] = share
        context = dot(share, kv[near, LANES:])
        part0 = context[:TILE] * gate0
        part1 = context[TILE:] * gate1
        for pair in range(pairs):
            mixed[span, pair * LANES : (pair + 1) * LANES] = jnp.where(
                masks[pair][0], part0, jnp.where(masks[pair][1], part1, 0.0)
            ).astype(BF16)
        if tile % (tiles // 2) == tiles // 2 - 1:
            done = pl.ds((tile + 1 - tiles // 2), tiles // 2)
            copies.start("out", chance.at[done], chance_far.at[done])
    copies.start("out", glow, glow_far)
    copies.start("out", qsel, qsel_far)
    copies.start("out", mixed, mixed_far)
    copies.start("out", gates, gates_far)
    for at in range(0, rows, BIG):
        span = pl.ds(at, BIG)
        total = tok[span, :].astype(F32) + dot(mixed[span, :], wo[...])
        res[span, :] = total.astype(BF16)
        hat, _ = normed(total)
        low2[span, :] = (hat * as_row(gain2) + as_row(shift2)).astype(BF16)
        if (at + BIG) % (rows // 2) == 0:
            done = pl.ds(at + BIG - rows // 2, rows // 2)
            copies.start("out", low2.at[done, :], low2_far.at[done, :])
            copies.start("out", res.at[done, :], res_far.at[done, :])
    copies.finish()


def ffn_kernel(*refs, units, more):
    low2, glow, weights = refs[:3]
    at = 3
    if "cut" in more:
        mine = refs[at]
        at += 1
    if "rows" in more:
        out_in, second_in = refs[at : at + 2]
        at += 2
    if "weights" in more:
        contract_in, expand_in, bias_in = refs[at : at + 3]
        at += 3
    if "cut" in more:
        out, second, contract_out, keep_out, send_out, bias_out, hidden, grad, uncut = refs[at:]
    else:
        out, second, contract_out, expand_out, bias_out, hidden, grad = refs[at:]
    rows = low2.shape[0]
    contract = weights.at[:units, :]
    expand = weights.at[units + 16 :, :units]
    bias = weights[units : units + 1, :units].astype(F32)
    bias_sum = bias_in[...] if "weights" in more else jnp.zeros((1, units), F32)
    for first in range(0, rows, BIG):
        span = pl.ds(first, BIG)
        preact = dot(low2[span, :], expand[...]) + bias
        cumulative = 0.5 * (1.0 + lax.erf(preact * (1.0 / math.sqrt(2.0))))
        bell = jnp.exp(-0.5 * preact * preact) * (1.0 / math.sqrt(2.0 * math.pi))
        high = (preact * cumulative).astype(BF16)
        hidden[span, :] = high
        slope = cumulative + preact * bell
        low_grad = (dot_nt(glow[span, :], contract[...]) * slope).astype(BF16)
        grad[span, :] = low_grad
        bias_sum += row_sum(low_grad.astype(F32))
        out_part = dot(high, contract[...])
        second_part = dot_nt(low_grad, expand[...])
        if "rows" in more:
            out_part += out_in[span, :].astype(F32)
            second_part += second_in[span, :].astype(F32)
        out[span, :] = out_part.astype(out.dtype)
        second[span, :] = second_part.astype(second.dtype)
    contract_sum = dot_tn(hidden[...], glow[...])
    expand_sum = dot_tn(low2[...], grad[...])
    if "weights" in more:
        contract_sum += contract_in[...]
        expand_sum += expand_in[...]
    contract_out[...] = contract_sum.astype(contract_out.dtype)
    bias_out[...] = bias_sum
    if "cut" in more:
        half = uncut.shape[0] // 2
        uncut[...] = expand_sum.astype(uncut.dtype)
        keep_out[...] = uncut[pl.ds(pl.multiple_of(mine[0] * half, half), half), :]
        send_out[...] = uncut[pl.ds(pl.multiple_of((1 - mine[0]) * half, half), half), :]
    else:
        expand_out[...] = expand_sum.astype(expand_out.dtype)


def ffn(rows_far, low2, glow, weights, weights_far, units, rows_in=None, weights_in=None,
        rows_out=("far", "far"), cut=None, carry="near"):
    rows, width = low2.shape
    more = []
    operands = [low2, glow, weights]
    spaces = [rows_far, rows_far, weights_far]
    if cut is not None:
        more.append("cut")
        operands.append(cut)
        spaces.append("scalar")
    if rows_in is not None:
        more.append("rows")
        operands += rows_in
        spaces += ["far" if rows_far else "near"] * 2
    if weights_in is not None:
        more.append("weights")
        operands += weights_in
        spaces += [carry, carry, "near"]
    scratch = [pltpu.VMEM((rows, units), BF16), pltpu.VMEM((rows, units), BF16)]
    if cut is None:
        sums = [
            jax.ShapeDtypeStruct((units, width), F32), jax.ShapeDtypeStruct((width, units), F32)
        ]
        sums_out = [carry, carry]
    else:
        sums = [jax.ShapeDtypeStruct((units, width), BF16)]
        sums += [jax.ShapeDtypeStruct((width // 2, units), BF16)] * 2
        sums_out = ["far", "far", "far"]
        scratch.append(pltpu.VMEM((width, units), BF16))
    outs = placed_call(
        functools.partial(ffn_kernel, units=units, more=tuple(more)),
        "ffn",
        operands,
        spaces,
        [jax.ShapeDtypeStruct((rows, width), BF16)] * 2
        + sums
        + [jax.ShapeDtypeStruct((1, units), F32)],
        list(rows_out) + sums_out + ["near"],
        scratch,
    )
    return list(outs[:2]), list(outs[2:])


def back_kernel(
    place, second_own, second_got, unit_own, unit_peers,
    res, glow, wo, gates, mixed, kv, chance, qsel, tok, wq, wkv,
    gain1, shift1, gain2, router,
    tok_grad, keep, send,
    packed, low1, grad_res, grad_mixed, grad_q, grad_log, key_sum, value_sum, vectors,
):
    rows, width = tok.shape
    tiles = rows // TILE
    pairs = width // LANES
    scale = (wkv.shape[1] // 2) ** -0.5
    experts = router.shape[0]
    gain_one, gain_two = as_row(gain1), as_row(gain2)
    gain2_sum = shift2_sum = bias_sum = jnp.zeros((1, width), F32)
    for at in range(0, rows, BIG):
        span = pl.ds(at, BIG)
        hat, inverse = normed(res[span, :].astype(F32))
        second = second_own[span, :].astype(F32) + second_got[span, :].astype(F32)
        gain2_sum += row_sum(second * hat)
        shift2_sum += row_sum(second)
        outer = glow[span, :].astype(F32)
        bias_sum += row_sum(outer)
        grad = outer + norm_back(second, gain_two, hat, inverse)
        grad_res[span, :] = grad
        grad_mixed[span, :] = dot_nt(grad.astype(BF16), wo[...])
    packed[:, width : 2 * width] = dot_tn(mixed[...], grad_res[...].astype(BF16)).astype(BF16)
    key_sum[...] = jnp.zeros_like(key_sum)
    value_sum[...] = jnp.zeros_like(value_sum)
    for tile in range(tiles):
        at = tile * TILE
        span = pl.ds(at, TILE)
        column = jnp.transpose(gates[:, at : at + TILE])
        gate0, gate1 = column[:, 0:1], column[:, 1:2]
        first_id, second_id = column[:, 2:3], column[:, 3:4]
        masks = pair_masks(first_id, second_id, pairs)
        g0 = jnp.zeros((TILE, LANES), F32)
        g1 = jnp.zeros((TILE, LANES), F32)
        use0 = jnp.zeros((TILE, LANES), F32)
        use1 = jnp.zeros((TILE, LANES), F32)
        for pair in range(pairs):
            lanes = slice(pair * LANES, (pair + 1) * LANES)
            block = grad_mixed[span, lanes]
            both = block * mixed[span, lanes].astype(F32)
            g0 = jnp.where(masks[pair][0], block, g0)
            g1 = jnp.where(masks[pair][1], block, g1)
            use0 = jnp.where(masks[pair][0], both, use0)
            use1 = jnp.where(masks[pair][1], both, use1)
        use0 = jnp.sum(use0, axis=-1, keepdims=True)
        use1 = jnp.sum(use1, axis=-1, keepdims=True)
        turn = gate1 * use0 - gate0 * use1
        lane = lax.broadcasted_iota(jnp.int32, (TILE, LANES), 1).astype(F32)
        grad_log[span, :] = jnp.where(
            lane == first_id, turn, jnp.where(lane == second_id, -turn, 0.0)
        ).astype(BF16)
        grad_ctx = jnp.concatenate([g0 * gate0, g1 * gate1], axis=0).astype(BF16)
        delta = jnp.concatenate([use0, use1], axis=0)
        start, extent = window_of(tile, tiles)
        near = pl.ds(start, extent)
        grad_share = dot_nt(grad_ctx, kv[near, LANES:])
        share = chance[tile]
        raw = (share.astype(F32) * (grad_share - delta)).astype(BF16)
        grad_query = dot(raw, kv[near, :LANES]) * scale
        for pair in range(pairs):
            grad_q[span, pair * LANES : (pair + 1) * LANES] = jnp.where(
                masks[pair][0],
                grad_query[:TILE],
                jnp.where(masks[pair][1], grad_query[TILE:], 0.0),
            ).astype(BF16)
        key_sum[near, :] += dot_tn(raw, qsel[tile])
        value_sum[near, :] += dot_tn(share, grad_ctx)
    keys, values = key_sum[...], value_sum[...]
    keys = keys + pltpu.roll(keys, LANES // 2, 1)
    values = values + pltpu.roll(values, LANES // 2, 1)
    half_lane = lax.broadcasted_iota(jnp.int32, (rows, LANES), 1) < LANES // 2
    grad_kv = jnp.where(half_lane, keys, values).astype(BF16)
    gain1_sum = shift1_sum = jnp.zeros((1, width), F32)
    for at in range(0, rows, BIG):
        span = pl.ds(at, BIG)
        hat, inverse = normed(tok[span, :].astype(F32))
        low1[span, :] = (hat * gain_one + as_row(shift1)).astype(BF16)
        grad = (
            dot_nt(grad_q[span, :], wq[...])
            + dot_nt(grad_kv[at : at + BIG], wkv[...])
            + dot(grad_log[span, :experts], router[...])
        )
        gain1_sum += row_sum(grad * hat)
        shift1_sum += row_sum(grad)
        tok_grad[span, :] = (grad_res[span, :] + norm_back(grad, gain_one, hat, inverse)).astype(
            BF16
        )
    packed[:, :width] = dot_tn(low1[...], grad_q[...]).astype(BF16)
    packed[:, 2 * width : 2 * width + LANES] = dot_tn(low1[...], grad_kv).astype(BF16)
    vectors[...] = jnp.zeros_like(vectors)
    sums = (gain1_sum, shift1_sum, gain2_sum, shift2_sum, bias_sum)
    for at, values in enumerate(sums):
        vectors[VECTOR_ROW + at : VECTOR_ROW + at + 1, :] = values
    units = unit_own.shape[1]
    own = place[0]
    for step in range(unit_peers.shape[0] + 1):
        owner = own ^ (2 * step)
        part = unit_own[...] if step == 0 else unit_peers[step - 1 : step, :]
        vectors[pl.ds(VECTOR_ROW + len(sums) + owner, 1), :units] = part
    packed[:, 2 * width + LANES :] = (
        dot_tn(low1[...], grad_log[...]) + jnp.transpose(vectors[...])
    ).astype(BF16)
    half = width // 2
    mine = own % 2
    keep[...] = packed[pl.ds(pl.multiple_of(mine * half, half), half), :]
    send[...] = packed[pl.ds(pl.multiple_of((1 - mine) * half, half), half), :]


def unpack_kernel(place, mine, other, gain1, shift1, router, query, output, keyval, gain2, shift2, unit, bias):
    half, width = mine.shape[0], query.shape[1]
    for end, values in ((place[0] % 2, mine), (1 - place[0] % 2, other)):
        span = pl.ds(pl.multiple_of(end * half, half), half)
        query[span, :] = values[:, :width].astype(F32)
        output[span, :] = values[:, width : 2 * width].astype(F32)
        keyval[span, :] = values[:, 2 * width : 2 * width + LANES].astype(F32)
        router[span, :] = values[:, 2 * width + LANES :].astype(F32)
    rows = jnp.transpose(router[...])
    for at, target in enumerate((gain1, shift1, gain2, shift2, bias)):
        target[...] = rows[VECTOR_ROW + at : VECTOR_ROW + at + 1, :]
    owner = lax.broadcasted_iota(jnp.int32, rows.shape, 0) - (VECTOR_ROW + 5)
    unit[...] = jnp.sum(jnp.where(owner == place[0], rows, 0.0), axis=0, keepdims=True)[
        :, : unit.shape[1]
    ]


def far_call(kernel, name, near, far, out_shape, scratch, copies):
    buffers = [pltpu.VMEM(item.shape, item.dtype) for item in list(far) + list(out_shape)]
    return pl.pallas_call(
        kernel,
        out_shape=[pltpu.HBM(item.shape, item.dtype) for item in out_shape],
        in_specs=[pl.BlockSpec(memory_space=pltpu.VMEM)] * len(near)
        + [pl.BlockSpec(memory_space=pl.ANY)] * len(far),
        out_specs=[pl.BlockSpec(memory_space=pl.ANY)] * len(out_shape),
        scratch_shapes=buffers + scratch + [pltpu.SemaphoreType.DMA((copies,))],
        compiler_params=pltpu.CompilerParams(vmem_limit_bytes=VMEM_LIMIT),
        cost_estimate=pl.CostEstimate(flops=1000, bytes_accessed=1000, transcendentals=0),
        name=name,
    )(
        *[pltpu.with_memory_space_constraint(item, pltpu.HBM) for item in near],
        *[pltpu.with_memory_space_constraint(item, pltpu.HBM) for item in far],
    )


def placed_call(kernel, name, operands, spaces, out_shape, out_spaces, scratch):
    where = {"far": pltpu.HBM, "near": pltpu.VMEM}
    lies = [pltpu.SMEM if space == "scalar" else pltpu.VMEM for space in spaces]
    operands = [
        pltpu.with_memory_space_constraint(item, where[space]) if space in where else item
        for item, space in zip(operands, spaces)
    ]
    results = [
        where[space](item.shape, item.dtype) if space in where else item
        for item, space in zip(out_shape, out_spaces)
    ]
    return pl.pallas_call(
        kernel,
        out_shape=results,
        in_specs=[pl.BlockSpec(memory_space=space) for space in lies],
        out_specs=[pl.BlockSpec(memory_space=pltpu.VMEM)] * len(results),
        scratch_shapes=scratch,
        compiler_params=pltpu.CompilerParams(vmem_limit_bytes=VMEM_LIMIT),
        cost_estimate=pl.CostEstimate(flops=1000, bytes_accessed=1000, transcendentals=0),
        name=name,
    )(*operands)


def swap(values, bit, devices):
    return lax.ppermute(values, AXES, [(at, at ^ bit) for at in range(devices)])


def halves(values, mine):
    size = values.shape[0] // 2
    keep = lax.dynamic_slice_in_dim(values, mine * size, size, 0)
    send = lax.dynamic_slice_in_dim(values, (1 - mine) * size, size, 0)
    return keep, send


def add_low(left, right):
    return (left.astype(F32) + right.astype(F32)).astype(BF16)


def scatter_sum(values, bits, place, devices, cut=None):
    if not bits:
        return values
    mines = [(place // bit) % 2 for bit in bits]
    keep, send = halves(values, mines[0]) if cut is None else cut
    for at, bit in enumerate(bits):
        got = swap(send, bit, devices)
        if at + 1 < len(bits):
            (keep, send), (keep_got, send_got) = (
                halves(item, mines[at + 1]) for item in (keep, got)
            )
            send = add_low(send, send_got)
            keep = add_low(keep, keep_got)
        else:
            values = add_low(keep, got)
    return values


def all_sum(values, bits, place, devices, whole=1):
    cut, full = bits[: len(bits) - whole], bits[len(bits) - whole :]
    values = scatter_sum(values, cut, place, devices)
    values = whole_sum(values, full, devices)
    return gather(values, cut, place, devices)


def whole_sum(values, bits, devices):
    for bit in bits:
        values = add_low(values, swap(values, bit, devices))
    return values


def joined(values, got, mine):
    return jnp.where(
        mine == 0,
        jnp.concatenate([values, got], axis=0),
        jnp.concatenate([got, values], axis=0),
    )


def gather(values, bits, place, devices):
    for bit in reversed(bits):
        values = joined(values, swap(values, bit, devices), (place // bit) % 2)
    return values


def shards(
    n_dp,
    n_mp,
    tokens,
    sentence_ids,
    validity,
    expert_ids,
    cotangent,
    first_gain,
    first_shift,
    router,
    query_weight,
    output_weight,
    keyval_weight,
    second_gain,
    second_shift,
    expand_weight,
    expand_bias,
    contract_weight,
    contract_bias,
):
    devices = n_dp * n_mp
    rows, width = tokens.shape
    units = expand_weight.shape[1]
    tiles = rows // TILE
    _, extent = window_of(0, tiles)
    place = lax.axis_index(AXES)
    mp_place = lax.axis_index("mp")

    def row(vector):
        return vector.reshape(1, -1)

    def shape(*dims, dtype=BF16):
        return jax.ShapeDtypeStruct(dims, dtype)

    bias_rows = jnp.broadcast_to(jnp.pad(expand_bias, (0, width - units))[None], (16, width))
    wide_expand = jnp.pad(expand_weight, ((0, 0), (0, width - units)))
    own = jnp.concatenate([contract_weight, bias_rows, wide_expand], axis=0)
    turned_router = router.T
    chips = n_mp // 2
    others = [swap(own, 2 * step, devices) for step in range(1, chips)]
    res, low2, glow, mixed, qsel, kv, chance, gates = far_call(
        attend_kernel,
        "attend",
        [
            row(sentence_ids), row(validity), expert_ids.T, first_gain, first_shift, second_gain,
            second_shift, turned_router,
        ],
        [tokens, query_weight, keyval_weight, cotangent, output_weight],
        [
            shape(rows, width),
            shape(rows, width),
            shape(rows, width),
            shape(rows, width),
            shape(tiles, 2 * TILE, LANES),
            shape(rows, 2 * LANES),
            shape(tiles, 2 * TILE, extent),
            shape(8, rows, dtype=F32),
        ],
        [pltpu.VMEM((rows, width), BF16), pltpu.VMEM((rows, router.shape[1]), F32)],
        20,
    )
    low2_pair = swap(low2, 1, devices)
    glow_pair = swap(glow, 1, devices)
    dp_bits = [n_mp << at for at in range(n_dp.bit_length() - 1)]
    mp_bits = [1 << at for at in range(n_mp.bit_length() - 1)]
    first_bit = dp_bits[min(1, len(dp_bits) - 1)]
    later_bits = [bit for bit in dp_bits if bit != first_bit]
    first_mine = jnp.full((1,), (place // first_bit) % 2, jnp.int32)
    rows_own, grads_own = ffn("far", low2, glow, own, "far", units, carry="far")
    rows_pair, grads_own = ffn(
        None, low2_pair, glow_pair, own, "far", units, weights_in=grads_own, rows_out=(None, None),
        cut=first_mine, carry="far",
    )
    contract_sum, expand_keep, expand_send, unit_own = grads_own
    unit_peers = []
    waiting = []
    for step in range(1, chips):
        final = step == chips - 1
        rows_pair, grads = ffn(
            None,
            low2_pair,
            glow_pair,
            others[step - 1],
            None,
            units,
            rows_in=rows_pair,
            rows_out=(None, None),
            carry="far",
        )
        if final:
            out_got, second_got = (swap(item, 1, devices) for item in rows_pair)
        rows_own, grads = ffn(
            "far",
            low2,
            glow,
            others[step - 1],
            None,
            units,
            rows_in=rows_own,
            weights_in=grads,
            rows_out=("far", "near" if final else "far"),
            cut=first_mine,
            carry="far",
        )
        contract_part, keep, send, unit_part = grads
        unit_peers.append(unit_part)
        contract_got = swap(contract_part, 2 * step, devices)
        waiting.append((contract_got, keep, swap(send, first_bit, devices)))
    expand_got = swap(expand_send, first_bit, devices)
    scalars = jnp.full((1,), mp_place, jnp.int32)
    tok_grad, keep, send = placed_call(
        back_kernel,
        "back",
        [
            scalars, rows_own[1], second_got, unit_own, jnp.concatenate(unit_peers, axis=0),
            res, glow, output_weight, gates, mixed, kv, chance, qsel, tokens, query_weight,
            keyval_weight, first_gain, first_shift, second_gain, turned_router,
        ],
        ["scalar", "near", None, None, None] + ["far"] * 15,
        [shape(rows, width)] + [shape(width // 2, 2 * width + 2 * LANES)] * 2,
        ["far", "near", "near"],
        [
            pltpu.VMEM((width, 2 * width + 2 * LANES), BF16),
            pltpu.VMEM((rows, width), BF16),
            pltpu.VMEM((rows, width), F32),
            pltpu.VMEM((rows, width), F32),
            pltpu.VMEM((rows, width), BF16),
            pltpu.VMEM((rows, LANES), BF16),
            pltpu.VMEM((rows, LANES), F32),
            pltpu.VMEM((rows, LANES), F32),
            pltpu.VMEM((LANES, width), F32),
        ],
    )
    send, expand_got, waiting = lax.optimization_barrier((send, expand_got, waiting))
    expand_sum = add_low(expand_keep, expand_got)
    for step in range(1, chips):
        contract_got, peer_keep, peer_got = waiting[step - 1]
        contract_sum = add_low(contract_sum, contract_got)
        expand_part = add_low(peer_keep, peer_got)
        expand_sum = add_low(expand_sum, swap(expand_part, 2 * step, devices))
    order = mp_bits + dp_bits
    cut, full = order[:-2], order[-2:]
    packed = scatter_sum(None, cut, place, devices, (keep, send))
    layer = (
        res.astype(F32) + rows_own[0].astype(F32) + out_got.astype(F32) + contract_bias.astype(F32)
    ).astype(BF16)
    contract_grad = all_sum(contract_sum, dp_bits, place, devices).astype(F32)
    expand_sum = all_sum(expand_sum, later_bits, place, devices)
    expand_grad = gather(expand_sum, [first_bit], place, devices).astype(F32)
    packed = gather(whole_sum(packed, full, devices), cut[1:], place, devices)
    other = swap(packed, mp_bits[0], devices)
    square = shape(width, width, dtype=F32)
    line = shape(1, width, dtype=F32)
    (
        gain1_grad, shift1_grad, router_grad, query_grad, output_grad, keyval_grad, gain2_grad,
        shift2_grad, unit_grad, bias_grad,
    ) = placed_call(
        unpack_kernel,
        "unpack",
        [scalars, packed, other],
        ["scalar", None, None],
        [
            line, line, shape(width, LANES, dtype=F32), square, square,
            shape(width, LANES, dtype=F32), line, line, shape(1, units, dtype=F32), line,
        ],
        [None] * 10,
        [],
    )
    return (
        layer,
        tok_grad,
        gain1_grad[0],
        shift1_grad[0],
        router_grad[:, : router.shape[1]],
        query_grad,
        output_grad,
        keyval_grad,
        gain2_grad[0],
        shift2_grad[0],
        expand_grad,
        unit_grad[0],
        contract_grad,
        bias_grad[0],
    )


def solution(mesh):
    tokens_spec = P(AXES, None)
    placed = (
        tokens_spec,
        P(AXES),
        P(AXES),
        tokens_spec,
        tokens_spec,
        P(),
        P(),
        P(),
        P(),
        P(),
        P(),
        P(),
        P(),
        P(None, "mp"),
        P("mp"),
        P("mp", None),
        P(),
    )
    return jax.shard_map(
        functools.partial(shards, mesh.shape["dp"], mesh.shape["mp"]),
        mesh=mesh,
        in_specs=placed,
        out_specs=(
            tokens_spec,
            tokens_spec,
            P(),
            P(),
            P(),
            P(),
            P(),
            P(),
            P(),
            P(),
            P(None, "mp"),
            P("mp"),
            P("mp", None),
            P(),
        ),
        check_vma=False,
    )
```

```python
import functools
import math

import jax
import jax.numpy as jnp
from jax import lax
from jax.experimental import pallas as pl
from jax.experimental.pallas import tpu as pltpu
from jax.sharding import PartitionSpec as P

F32 = jnp.float32
BF16 = jnp.bfloat16
epsilon = 1e-05
AXES = ("dp", "mp")
TILE = 128
BIG = 256
VMEM_LIMIT = 36 << 20
LANES = 128
VECTOR_ROW = 8


def dot(left, right):
    return lax.dot_general(left, right, (((1,), (0,)), ((), ())), preferred_element_type=F32)


def dot_nt(left, right):
    return lax.dot_general(left, right, (((1,), (1,)), ((), ())), preferred_element_type=F32)


def dot_tn(left, right):
    return lax.dot_general(left, right, (((0,), (0,)), ((), ())), preferred_element_type=F32)


def normed(rows_in):
    middle = jnp.mean(rows_in, axis=-1, keepdims=True)
    center = rows_in - middle
    inverse = lax.rsqrt(jnp.mean(center * center, axis=-1, keepdims=True) + epsilon)
    return center * inverse, inverse


def norm_back(grad_normed, gain, normed_hat, inverse):
    scaled = grad_normed * gain
    mean_one = jnp.mean(scaled, axis=-1, keepdims=True)
    mean_two = jnp.mean(scaled * normed_hat, axis=-1, keepdims=True)
    return inverse * (scaled - mean_one - normed_hat * mean_two)


def as_row(vector):
    return vector[...].astype(F32).reshape(1, -1)


def row_sum(values):
    return jnp.sum(values, axis=0, keepdims=True)


def pair_masks(first_id, second_id, pairs):
    half = (lax.broadcasted_iota(jnp.int32, (TILE, LANES), 1) >= LANES // 2).astype(F32)
    low = first_id - half
    high = second_id - half
    return [(low == 2.0 * pair, high == 2.0 * pair) for pair in range(pairs)]


def window_of(tile, tiles):
    width = min(3, tiles)
    return min(max(tile - 1, 0), tiles - width) * TILE, width * TILE


class Copies:
    def __init__(self, semaphores):
        self.semaphores = semaphores
        self.used = 0
        self.pending = {}

    def start(self, name, source, target):
        copy = pltpu.make_async_copy(source, target, self.semaphores.at[self.used])
        self.used += 1
        copy.start()
        self.pending.setdefault(name, []).append(copy)

    def wait(self, *names):
        for name in names:
            for copy in self.pending.pop(name, ()):
                copy.wait()

    def finish(self):
        self.wait(*list(self.pending))


def attend_kernel(
    sent, valid, expert, gain1, shift1, gain2, shift2, router,
    tok_far, wq_far, wkv_far, cot_far, wo_far,
    res_far, low2_far, glow_far, mixed_far, qsel_far, kv_far, chance_far, gates_far,
    tok, wq, wkv, cot, wo,
    res, low2, glow, mixed, qsel, kv, chance, gates,
    queries, logits, semaphores,
):
    rows, width = tok.shape
    tiles = rows // TILE
    pairs = width // LANES
    scale = (wkv.shape[1] // 2) ** -0.5
    copies = Copies(semaphores)
    copies.start("tok", tok_far, tok)
    copies.start("wq", wq_far, wq)
    copies.start("wkv", wkv_far, wkv)
    copies.start("cot", cot_far, cot)
    copies.start("wo", wo_far, wo)
    half_lane = lax.broadcasted_iota(jnp.int32, (BIG, LANES), 1) < LANES // 2
    copies.wait("tok", "wq", "wkv")
    for at in range(0, rows, BIG):
        span = pl.ds(at, BIG)
        hat, _ = normed(tok[span, :].astype(F32))
        low = (hat * as_row(gain1) + as_row(shift1)).astype(BF16)
        queries[span, :] = dot(low, wq[...]).astype(BF16)
        logits[span, :] = dot_nt(low, router[...])
        both = dot(low, wkv[...])
        turned = pltpu.roll(both, LANES // 2, 1)
        kv[span, :LANES] = jnp.where(half_lane, both, turned).astype(BF16)
        kv[span, LANES:] = jnp.where(half_lane, turned, both).astype(BF16)
    copies.start("out", kv, kv_far)
    copies.wait("cot", "wo")
    for tile in range(tiles):
        at = tile * TILE
        span = pl.ds(at, TILE)
        meta = jnp.concatenate(
            [
                sent[:, at : at + TILE],
                valid[:, at : at + TILE],
                expert[:, at : at + TILE],
                jnp.zeros((4, TILE), jnp.int32),
            ],
            axis=0,
        ).astype(F32)
        column = jnp.transpose(meta)
        own_sent, own_valid = column[:, 0:1], column[:, 1:2]
        first_id, second_id = column[:, 2:3], column[:, 3:4]
        glow[span, :] = jnp.where(own_valid > 0.5, cot[span, :].astype(F32), 0.0).astype(BF16)
        scored = logits[span, :]
        slot = lax.broadcasted_iota(jnp.int32, scored.shape, 1).astype(F32)
        pick0 = jnp.sum(jnp.where(slot == first_id, scored, 0.0), axis=-1, keepdims=True)
        pick1 = jnp.sum(jnp.where(slot == second_id, scored, 0.0), axis=-1, keepdims=True)
        most = jnp.maximum(pick0, pick1)
        raise0, raise1 = jnp.exp(pick0 - most), jnp.exp(pick1 - most)
        gate0 = raise0 / (raise0 + raise1)
        gate1 = raise1 / (raise0 + raise1)
        lane = lax.broadcasted_iota(jnp.int32, (TILE, 8), 1)
        gates[:, at : at + TILE] = jnp.transpose(
            jnp.where(
                lane == 0,
                gate0,
                jnp.where(lane == 1, gate1, jnp.where(lane == 2, first_id, second_id)),
            )
        )
        masks = pair_masks(first_id, second_id, pairs)
        q0 = jnp.zeros((TILE, LANES), F32)
        q1 = jnp.zeros((TILE, LANES), F32)
        for pair in range(pairs):
            block = queries[span, pair * LANES : (pair + 1) * LANES].astype(F32)
            q0 = jnp.where(masks[pair][0], block, q0)
            q1 = jnp.where(masks[pair][1], block, q1)
        picked = (jnp.concatenate([q0, q1], axis=0) * scale).astype(BF16)
        qsel[tile] = picked
        start, extent = window_of(tile, tiles)
        near = pl.ds(start, extent)
        scores = dot_nt(picked, kv[near, :LANES])
        same = own_sent == sent[:, start : start + extent].astype(F32)
        same = jnp.concatenate([same, same], axis=0)
        scores = jnp.where(same, scores, -1e30)
        weights = jnp.exp(scores - jnp.max(scores, axis=-1, keepdims=True))
        share = (weights * (1.0 / jnp.sum(weights, axis=-1, keepdims=True))).astype(BF16)
        chance[tile] = share
        context = dot(share, kv[near, LANES:])
        part0 = context[:TILE] * gate0
        part1 = context[TILE:] * gate1
        for pair in range(pairs):
            mixed[span, pair * LANES : (pair + 1) * LANES] = jnp.where(
                masks[pair][0], part0, jnp.where(masks[pair][1], part1, 0.0)
            ).astype(BF16)
        if tile % (tiles // 2) == tiles // 2 - 1:
            done = pl.ds((tile + 1 - tiles // 2), tiles // 2)
            copies.start("out", chance.at[done], chance_far.at[done])
    copies.start("out", glow, glow_far)
    copies.start("out", qsel, qsel_far)
    copies.start("out", mixed, mixed_far)
    copies.start("out", gates, gates_far)
    for at in range(0, rows, BIG):
        span = pl.ds(at, BIG)
        total = tok[span, :].astype(F32) + dot(mixed[span, :], wo[...])
        res[span, :] = total.astype(BF16)
        hat, _ = normed(total)
        low2[span, :] = (hat * as_row(gain2) + as_row(shift2)).astype(BF16)
        if (at + BIG) % (rows // 2) == 0:
            done = pl.ds(at + BIG - rows // 2, rows // 2)
            copies.start("out", low2.at[done, :], low2_far.at[done, :])
            copies.start("out", res.at[done, :], res_far.at[done, :])
    copies.finish()


def ffn_kernel(*refs, units, more):
    low2, glow, weights = refs[:3]
    at = 3
    if "rows" in more:
        out_in, second_in = refs[at : at + 2]
        at += 2
    if "weights" in more:
        contract_in, expand_in, bias_in = refs[at : at + 3]
        at += 3
    if "final" in more:
        out, second, contract_out, folded_out, bias_out, hidden, grad = refs[at:]
    else:
        out, second, contract_out, expand_out, bias_out, hidden, grad = refs[at:]
    rows = low2.shape[0]
    contract = weights.at[:units, :]
    expand = weights.at[units + 16 :, :units]
    bias = weights[units : units + 1, :units].astype(F32)
    bias_sum = bias_in[...] if "weights" in more else jnp.zeros((1, units), F32)
    for first in range(0, rows, BIG):
        span = pl.ds(first, BIG)
        preact = dot(low2[span, :], expand[...]) + bias
        cumulative = 0.5 * (1.0 + lax.erf(preact * (1.0 / math.sqrt(2.0))))
        bell = jnp.exp(-0.5 * preact * preact) * (1.0 / math.sqrt(2.0 * math.pi))
        high = (preact * cumulative).astype(BF16)
        hidden[span, :] = high
        slope = cumulative + preact * bell
        low_grad = (dot_nt(glow[span, :], contract[...]) * slope).astype(BF16)
        grad[span, :] = low_grad
        bias_sum += row_sum(low_grad.astype(F32))
        out_part = dot(high, contract[...])
        second_part = dot_nt(low_grad, expand[...])
        if "rows" in more:
            out_part += out_in[span, :].astype(F32)
            second_part += second_in[span, :].astype(F32)
        out[span, :] = out_part.astype(out.dtype)
        second[span, :] = second_part.astype(second.dtype)
    contract_sum = dot_tn(hidden[...], glow[...])
    expand_sum = dot_tn(low2[...], grad[...])
    if "weights" in more:
        contract_sum += contract_in[...].astype(F32)
        expand_sum += expand_in[...].astype(F32)
    bias_out[...] = bias_sum
    if "final" in more:
        contract_out[...] = contract_sum.astype(contract_out.dtype)
        for at in range(0, expand_sum.shape[0], units):
            block = expand_sum[at : at + units, :]
            folded_out[:, at : at + units] = block.astype(folded_out.dtype)
    else:
        contract_out[...] = contract_sum.astype(contract_out.dtype)
        expand_out[...] = expand_sum.astype(expand_out.dtype)


def ffn(rows_far, low2, glow, weights, weights_far, units, rows_in=None, weights_in=None,
        rows_out=("far", "far"), final=False, carry="far"):
    rows, width = low2.shape
    more = []
    operands = [low2, glow, weights]
    spaces = [rows_far, rows_far, weights_far]
    if final:
        more.append("final")
    if rows_in is not None:
        more.append("rows")
        operands += rows_in
        spaces += ["far" if rows_far else "near"] * 2
    if weights_in is not None:
        more.append("weights")
        operands += weights_in
        spaces += [carry, carry, "near"]
    scratch = [pltpu.VMEM((rows, units), BF16), pltpu.VMEM((rows, units), BF16)]
    if final:
        sums = [jax.ShapeDtypeStruct((units, width), BF16)] * 2
    else:
        sums = [
            jax.ShapeDtypeStruct((units, width), BF16), jax.ShapeDtypeStruct((width, units), BF16)
        ]
    sums_out = [carry] * len(sums)
    outs = placed_call(
        functools.partial(ffn_kernel, units=units, more=tuple(more)),
        "ffn",
        operands,
        spaces,
        [jax.ShapeDtypeStruct((rows, width), BF16)] * 2
        + sums
        + [jax.ShapeDtypeStruct((1, units), F32)],
        list(rows_out) + sums_out + ["near"],
        scratch,
    )
    return list(outs[:2]), list(outs[2:])


def back_kernel(
    place, second_own, second_got, unit_own, unit_peers,
    res, glow, wo, gates, mixed, kv, chance, qsel, tok, wq, wkv,
    gain1, shift1, gain2, router,
    tok_grad, keep, send,
    packed, low1, grad_res, grad_mixed, grad_q, grad_log, key_sum, value_sum, vectors,
):
    rows, width = tok.shape
    tiles = rows // TILE
    pairs = width // LANES
    scale = (wkv.shape[1] // 2) ** -0.5
    experts = router.shape[0]
    gain_one, gain_two = as_row(gain1), as_row(gain2)
    gain2_sum = shift2_sum = bias_sum = jnp.zeros((1, width), F32)
    for at in range(0, rows, BIG):
        span = pl.ds(at, BIG)
        hat, inverse = normed(res[span, :].astype(F32))
        second = second_own[span, :].astype(F32) + second_got[span, :].astype(F32)
        gain2_sum += row_sum(second * hat)
        shift2_sum += row_sum(second)
        outer = glow[span, :].astype(F32)
        bias_sum += row_sum(outer)
        grad = outer + norm_back(second, gain_two, hat, inverse)
        grad_res[span, :] = grad
        grad_mixed[span, :] = dot_nt(grad.astype(BF16), wo[...])
    packed[:, width : 2 * width] = dot_tn(mixed[...], grad_res[...].astype(BF16)).astype(BF16)
    key_sum[...] = jnp.zeros_like(key_sum)
    value_sum[...] = jnp.zeros_like(value_sum)
    for tile in range(tiles):
        at = tile * TILE
        span = pl.ds(at, TILE)
        column = jnp.transpose(gates[:, at : at + TILE])
        gate0, gate1 = column[:, 0:1], column[:, 1:2]
        first_id, second_id = column[:, 2:3], column[:, 3:4]
        masks = pair_masks(first_id, second_id, pairs)
        g0 = jnp.zeros((TILE, LANES), F32)
        g1 = jnp.zeros((TILE, LANES), F32)
        use0 = jnp.zeros((TILE, LANES), F32)
        use1 = jnp.zeros((TILE, LANES), F32)
        for pair in range(pairs):
            lanes = slice(pair * LANES, (pair + 1) * LANES)
            block = grad_mixed[span, lanes]
            both = block * mixed[span, lanes].astype(F32)
            g0 = jnp.where(masks[pair][0], block, g0)
            g1 = jnp.where(masks[pair][1], block, g1)
            use0 = jnp.where(masks[pair][0], both, use0)
            use1 = jnp.where(masks[pair][1], both, use1)
        use0 = jnp.sum(use0, axis=-1, keepdims=True)
        use1 = jnp.sum(use1, axis=-1, keepdims=True)
        turn = gate1 * use0 - gate0 * use1
        lane = lax.broadcasted_iota(jnp.int32, (TILE, LANES), 1).astype(F32)
        grad_log[span, :] = jnp.where(
            lane == first_id, turn, jnp.where(lane == second_id, -turn, 0.0)
        ).astype(BF16)
        grad_ctx = jnp.concatenate([g0 * gate0, g1 * gate1], axis=0).astype(BF16)
        delta = jnp.concatenate([use0, use1], axis=0)
        start, extent = window_of(tile, tiles)
        near = pl.ds(start, extent)
        grad_share = dot_nt(grad_ctx, kv[near, LANES:])
        share = chance[tile]
        raw = (share.astype(F32) * (grad_share - delta)).astype(BF16)
        grad_query = dot(raw, kv[near, :LANES]) * scale
        for pair in range(pairs):
            grad_q[span, pair * LANES : (pair + 1) * LANES] = jnp.where(
                masks[pair][0],
                grad_query[:TILE],
                jnp.where(masks[pair][1], grad_query[TILE:], 0.0),
            ).astype(BF16)
        key_sum[near, :] += dot_tn(raw, qsel[tile])
        value_sum[near, :] += dot_tn(share, grad_ctx)
    keys, values = key_sum[...], value_sum[...]
    keys = keys + pltpu.roll(keys, LANES // 2, 1)
    values = values + pltpu.roll(values, LANES // 2, 1)
    half_lane = lax.broadcasted_iota(jnp.int32, (rows, LANES), 1) < LANES // 2
    grad_kv = jnp.where(half_lane, keys, values).astype(BF16)
    gain1_sum = shift1_sum = jnp.zeros((1, width), F32)
    for at in range(0, rows, BIG):
        span = pl.ds(at, BIG)
        hat, inverse = normed(tok[span, :].astype(F32))
        low1[span, :] = (hat * gain_one + as_row(shift1)).astype(BF16)
        grad = (
            dot_nt(grad_q[span, :], wq[...])
            + dot_nt(grad_kv[at : at + BIG], wkv[...])
            + dot(grad_log[span, :experts], router[...])
        )
        gain1_sum += row_sum(grad * hat)
        shift1_sum += row_sum(grad)
        tok_grad[span, :] = (grad_res[span, :] + norm_back(grad, gain_one, hat, inverse)).astype(
            BF16
        )
    packed[:, :width] = dot_tn(low1[...], grad_q[...]).astype(BF16)
    packed[:, 2 * width : 2 * width + LANES] = dot_tn(low1[...], grad_kv).astype(BF16)
    vectors[...] = jnp.zeros_like(vectors)
    sums = (gain1_sum, shift1_sum, gain2_sum, shift2_sum, bias_sum)
    for at, values in enumerate(sums):
        vectors[VECTOR_ROW + at : VECTOR_ROW + at + 1, :] = values
    units = unit_own.shape[1]
    own = place[0]
    for step in range(unit_peers.shape[0] + 1):
        owner = own ^ (2 * step)
        part = unit_own[...] if step == 0 else unit_peers[step - 1 : step, :]
        vectors[pl.ds(VECTOR_ROW + len(sums) + owner, 1), :units] = part
    packed[:, 2 * width + LANES :] = (
        dot_tn(low1[...], grad_log[...]) + jnp.transpose(vectors[...])
    ).astype(BF16)
    half = width // 2
    mine = own % 2
    keep[...] = packed[pl.ds(pl.multiple_of(mine * half, half), half), :]
    send[...] = packed[pl.ds(pl.multiple_of((1 - mine) * half, half), half), :]


def unpack_kernel(
    place, mine, other,
    gain1, shift1, router, query, output, keyval, gain2, shift2, unit, bias,
    rest,
):
    half, width = mine.shape[0], query.shape[1]
    for end, values in ((place[0] % 2, mine), (1 - place[0] % 2, other)):
        span = pl.ds(pl.multiple_of(end * half, half), half)
        query[span, :] = values[:, :width].astype(F32)
        output[span, :] = values[:, width : 2 * width].astype(F32)
        keyval[span, :] = values[:, 2 * width : 2 * width + LANES].astype(F32)
        rest[span, :] = values[:, 2 * width + LANES :].astype(F32)
    rows = jnp.transpose(rest[...])
    router[...] = rows[: router.shape[0], :]
    for at, target in enumerate((gain1, shift1, gain2, shift2, bias)):
        target[...] = rows[VECTOR_ROW + at : VECTOR_ROW + at + 1, :]
    owner = lax.broadcasted_iota(jnp.int32, rows.shape, 0) - (VECTOR_ROW + 5)
    unit[...] = jnp.sum(jnp.where(owner == place[0], rows, 0.0), axis=0, keepdims=True)[
        :, : unit.shape[1]
    ]


def far_call(kernel, name, near, far, out_shape, scratch, copies):
    buffers = [pltpu.VMEM(item.shape, item.dtype) for item in list(far) + list(out_shape)]
    return pl.pallas_call(
        kernel,
        out_shape=[pltpu.HBM(item.shape, item.dtype) for item in out_shape],
        in_specs=[pl.BlockSpec(memory_space=pltpu.VMEM)] * len(near)
        + [pl.BlockSpec(memory_space=pl.ANY)] * len(far),
        out_specs=[pl.BlockSpec(memory_space=pl.ANY)] * len(out_shape),
        scratch_shapes=buffers + scratch + [pltpu.SemaphoreType.DMA((copies,))],
        compiler_params=pltpu.CompilerParams(vmem_limit_bytes=VMEM_LIMIT),
        cost_estimate=pl.CostEstimate(flops=1000, bytes_accessed=1000, transcendentals=0),
        name=name,
    )(
        *[pltpu.with_memory_space_constraint(item, pltpu.HBM) for item in near],
        *[pltpu.with_memory_space_constraint(item, pltpu.HBM) for item in far],
    )


def placed_call(kernel, name, operands, spaces, out_shape, out_spaces, scratch):
    where = {"far": pltpu.HBM, "near": pltpu.VMEM}
    lies = [pltpu.SMEM if space == "scalar" else pltpu.VMEM for space in spaces]
    operands = [
        pltpu.with_memory_space_constraint(item, where[space]) if space in where else item
        for item, space in zip(operands, spaces)
    ]
    results = [
        where[space](item.shape, item.dtype) if space in where else item
        for item, space in zip(out_shape, out_spaces)
    ]
    return pl.pallas_call(
        kernel,
        out_shape=results,
        in_specs=[pl.BlockSpec(memory_space=space) for space in lies],
        out_specs=[pl.BlockSpec(memory_space=pltpu.VMEM)] * len(results),
        scratch_shapes=scratch,
        compiler_params=pltpu.CompilerParams(vmem_limit_bytes=VMEM_LIMIT),
        cost_estimate=pl.CostEstimate(flops=1000, bytes_accessed=1000, transcendentals=0),
        name=name,
    )(*operands)


def swap(values, bit, devices):
    return lax.ppermute(values, AXES, [(at, at ^ bit) for at in range(devices)])


def halves(values, mine):
    size = values.shape[0] // 2
    keep = lax.dynamic_slice_in_dim(values, mine * size, size, 0)
    send = lax.dynamic_slice_in_dim(values, (1 - mine) * size, size, 0)
    return keep, send


def add_low(left, right):
    return (left.astype(F32) + right.astype(F32)).astype(BF16)


class Chain:
    def __init__(self, steps, place, devices):
        self.steps = list(steps)
        self.place, self.devices = place, devices
        self.values = self.keep = self.outgoing = None

    def mine(self, at):
        return (self.place // self.steps[at][1]) % 2

    def feed(self, values):
        self.values = values
        if self.steps and self.steps[0][0] == "cut":
            self.keep, self.outgoing = halves(values, self.mine(0))
        else:
            self.outgoing = values
        return self

    def feed_halves(self, keep, send):
        self.keep, self.outgoing = keep, send
        return self

    def send(self):
        return swap(self.outgoing, self.steps[0][1], self.devices)

    def take(self, got):
        kind = self.steps[0][0]
        if kind == "cut" and len(self.steps) > 1 and self.steps[1][0] == "cut":
            (keep, send), (keep_got, send_got) = (
                halves(item, self.mine(1)) for item in (self.keep, got)
            )
            self.outgoing = add_low(send, send_got)
            self.keep = add_low(keep, keep_got)
        else:
            if kind == "cut":
                values = add_low(self.keep, got)
            elif kind == "full":
                values = add_low(self.values, got)
            else:
                values = joined(self.values, got, self.mine(0))
            self.values = self.outgoing = values
        self.steps.pop(0)

    def run(self, steps):
        for _ in range(min(steps, len(self.steps))):
            self.take(self.send())
        return self.values


def plan(bits, whole=1):
    cut, full = bits[: len(bits) - whole], bits[len(bits) - whole :]
    return (
        [("cut", bit) for bit in cut]
        + [("full", bit) for bit in full]
        + [("join", bit) for bit in reversed(cut)]
    )


def sum_low(parts):
    return functools.reduce(jnp.add, [part.astype(F32) for part in parts]).astype(BF16)


def joined(values, got, mine):
    return jnp.where(
        mine == 0,
        jnp.concatenate([values, got], axis=0),
        jnp.concatenate([got, values], axis=0),
    )


def shards(
    n_dp,
    n_mp,
    tokens,
    sentence_ids,
    validity,
    expert_ids,
    cotangent,
    first_gain,
    first_shift,
    router,
    query_weight,
    output_weight,
    keyval_weight,
    second_gain,
    second_shift,
    expand_weight,
    expand_bias,
    contract_weight,
    contract_bias,
):
    devices = n_dp * n_mp
    rows, width = tokens.shape
    units = expand_weight.shape[1]
    tiles = rows // TILE
    _, extent = window_of(0, tiles)
    place = lax.axis_index(AXES)
    mp_place = lax.axis_index("mp")

    def row(vector):
        return vector.reshape(1, -1)

    def shape(*dims, dtype=BF16):
        return jax.ShapeDtypeStruct(dims, dtype)

    bias_rows = jnp.pad(expand_bias[None], ((0, 15), (0, width - units)))
    wide_expand = jnp.pad(expand_weight, ((0, 0), (0, width - units)))
    own = jnp.concatenate([contract_weight, bias_rows, wide_expand], axis=0)
    turned_router = router.T
    chips = n_mp // 2
    others = [swap(own, 2 * step, devices) for step in range(1, chips)]
    res, low2, glow, mixed, qsel, kv, chance, gates = far_call(
        attend_kernel,
        "attend",
        [
            row(sentence_ids), row(validity), expert_ids.T, first_gain, first_shift, second_gain,
            second_shift, turned_router,
        ],
        [tokens, query_weight, keyval_weight, cotangent, output_weight],
        [
            shape(rows, width),
            shape(rows, width),
            shape(rows, width),
            shape(rows, width),
            shape(tiles, 2 * TILE, LANES),
            shape(rows, 2 * LANES),
            shape(tiles, 2 * TILE, extent),
            shape(8, rows, dtype=F32),
        ],
        [pltpu.VMEM((rows, width), BF16), pltpu.VMEM((rows, router.shape[1]), F32)],
        20,
    )
    low2_pair = swap(low2, 1, devices)
    glow_pair = swap(glow, 1, devices)
    dp_bits = [n_mp << at for at in range(n_dp.bit_length() - 1)]
    mp_bits = [1 << at for at in range(n_mp.bit_length() - 1)]
    rows_own, grads_own = ffn("far", low2, glow, own, "far", units)
    rows_pair, grads_own = ffn(
        None, low2_pair, glow_pair, own, "far", units, weights_in=grads_own, rows_out=(None, None),
        final=True,
    )
    contract_sum, expand_sum, unit_own = grads_own
    unit_peers = []
    waiting = []
    for step in range(1, chips):
        final = step == chips - 1
        rows_pair, grads = ffn(
            None,
            low2_pair,
            glow_pair,
            others[step - 1],
            None,
            units,
            rows_in=rows_pair,
            rows_out=(None, None),
        )
        if final:
            out_got, second_got = (swap(item, 1, devices) for item in rows_pair)
        rows_own, grads = ffn(
            "far",
            low2,
            glow,
            others[step - 1],
            None,
            units,
            rows_in=rows_own,
            weights_in=grads,
            rows_out=("far", "near" if final else "far"),
            final=True,
        )
        unit_peers.append(grads[2])
        waiting.append([swap(item, 2 * step, devices) for item in grads[:2]])
    scalars = jnp.full((1,), mp_place, jnp.int32)
    tok_grad, keep, send = placed_call(
        back_kernel,
        "back",
        [
            scalars, rows_own[1], second_got, unit_own, jnp.concatenate(unit_peers, axis=0),
            res, glow, output_weight, gates, mixed, kv, chance, qsel, tokens, query_weight,
            keyval_weight, first_gain, first_shift, second_gain, turned_router,
        ],
        ["scalar", "near", None, None, None] + ["far"] * 15,
        [shape(rows, width)] + [shape(width // 2, 2 * width + 2 * LANES)] * 2,
        ["far", "near", "near"],
        [
            pltpu.VMEM((width, 2 * width + 2 * LANES), BF16),
            pltpu.VMEM((rows, width), BF16),
            pltpu.VMEM((rows, width), F32),
            pltpu.VMEM((rows, width), F32),
            pltpu.VMEM((rows, width), BF16),
            pltpu.VMEM((rows, LANES), BF16),
            pltpu.VMEM((rows, LANES), F32),
            pltpu.VMEM((rows, LANES), F32),
            pltpu.VMEM((LANES, width), F32),
        ],
    )
    order = mp_bits[:1] + dp_bits[:1] + mp_bits[1:] + dp_bits[1:]
    contract_got = [item[0] for item in waiting]
    expand_got = [item[1] for item in waiting]
    send, contract_got = lax.optimization_barrier((send, contract_got))
    first = Chain(plan(dp_bits[1:2] + dp_bits[:1] + dp_bits[2:]), place, devices)
    first.feed(sum_low([contract_sum, *contract_got]))
    second = Chain(plan(dp_bits), place, devices)
    chain = Chain(plan(order, 2)[:-1], place, devices).feed_halves(keep, send)
    for at in range(len(chain.steps)):
        got = chain.send()
        if at == 1:
            got, expand_got = lax.optimization_barrier((got, expand_got))
            second.feed(sum_low([expand_sum, *expand_got]))
        chain.take(got)
    packed = chain.values
    layer = (
        res.astype(F32) + rows_own[0].astype(F32) + out_got.astype(F32) + contract_bias.astype(F32)
    ).astype(BF16)
    contract_sum = first.run(len(first.steps))
    contract_grad = contract_sum.astype(F32)
    other = swap(packed, mp_bits[0], devices)
    square = shape(width, width, dtype=F32)
    line = shape(1, width, dtype=F32)
    unpacked = placed_call(
        unpack_kernel,
        "unpack",
        [scalars, packed, other],
        ["scalar", None, None],
        [
            line, line, shape(router.shape[1], width, dtype=F32), square, square,
            shape(width, LANES, dtype=F32), line, line, shape(1, units, dtype=F32), line,
        ],
        [None] * 10,
        [pltpu.VMEM((width, LANES), F32)],
    )
    second.run(len(second.steps) - 1)
    got, unpacked, contract_grad, layer = lax.optimization_barrier(
        (second.send(), unpacked, contract_grad, layer)
    )
    second.take(got)
    expand_sum = second.values
    expand_grad = jnp.concatenate(
        [expand_sum[:, at : at + units] for at in range(0, width, units)], axis=0
    ).astype(F32)
    (
        gain1_grad, shift1_grad, router_grad, query_grad, output_grad, keyval_grad, gain2_grad,
        shift2_grad, unit_grad, bias_grad,
    ) = unpacked
    return (
        layer,
        tok_grad,
        gain1_grad[0],
        shift1_grad[0],
        router_grad.T,
        query_grad,
        output_grad,
        keyval_grad,
        gain2_grad[0],
        shift2_grad[0],
        expand_grad,
        unit_grad[0],
        contract_grad,
        bias_grad[0],
    )


def solution(mesh):
    tokens_spec = P(AXES, None)
    placed = (
        tokens_spec,
        P(AXES),
        P(AXES),
        tokens_spec,
        tokens_spec,
        P(),
        P(),
        P(),
        P(),
        P(),
        P(),
        P(),
        P(),
        P(None, "mp"),
        P("mp"),
        P("mp", None),
        P(),
    )
    return jax.shard_map(
        functools.partial(shards, mesh.shape["dp"], mesh.shape["mp"]),
        mesh=mesh,
        in_specs=placed,
        out_specs=(
            tokens_spec,
            tokens_spec,
            P(),
            P(),
            P(),
            P(),
            P(),
            P(),
            P(),
            P(),
            P(None, "mp"),
            P("mp"),
            P("mp", None),
            P(),
        ),
        check_vma=False,
    )
```

```python
import functools
import math

import jax
import jax.numpy as jnp
from jax import lax
from jax.experimental import pallas as pl
from jax.experimental.pallas import tpu as pltpu
from jax.sharding import PartitionSpec as P

F32 = jnp.float32
BF16 = jnp.bfloat16
epsilon = 1e-05
AXES = ("dp", "mp")
TILE = 128
BIG = 256
VMEM_LIMIT = 36 << 20
LANES = 128
VECTOR_ROW = 8


def dot(left, right):
    return lax.dot_general(left, right, (((1,), (0,)), ((), ())), preferred_element_type=F32)


def dot_nt(left, right):
    return lax.dot_general(left, right, (((1,), (1,)), ((), ())), preferred_element_type=F32)


def dot_tn(left, right):
    return lax.dot_general(left, right, (((0,), (0,)), ((), ())), preferred_element_type=F32)


def normed(rows_in):
    middle = jnp.mean(rows_in, axis=-1, keepdims=True)
    center = rows_in - middle
    inverse = lax.rsqrt(jnp.mean(center * center, axis=-1, keepdims=True) + epsilon)
    return center * inverse, inverse


def norm_back(grad_normed, gain, normed_hat, inverse):
    scaled = grad_normed * gain
    mean_one = jnp.mean(scaled, axis=-1, keepdims=True)
    mean_two = jnp.mean(scaled * normed_hat, axis=-1, keepdims=True)
    return inverse * (scaled - mean_one - normed_hat * mean_two)


def as_row(vector):
    return vector[...].astype(F32).reshape(1, -1)


def row_sum(values):
    return jnp.sum(values, axis=0, keepdims=True)


def pair_masks(first_id, second_id, pairs):
    half = (lax.broadcasted_iota(jnp.int32, (TILE, LANES), 1) >= LANES // 2).astype(F32)
    low = first_id - half
    high = second_id - half
    return [(low == 2.0 * pair, high == 2.0 * pair) for pair in range(pairs)]


def window_of(tile, tiles):
    width = min(3, tiles)
    return min(max(tile - 1, 0), tiles - width) * TILE, width * TILE


def attend_kernel(
    sent, valid, expert, gain1, shift1, gain2, shift2, router, tok, wq, wkv, cot, wo,
    res, low2, glow, mixed, qsel, kv, chance, gates,
    queries, logits,
):
    rows, width = tok.shape
    tiles = rows // TILE
    pairs = width // LANES
    scale = (wkv.shape[1] // 2) ** -0.5
    half_lane = lax.broadcasted_iota(jnp.int32, (BIG, LANES), 1) < LANES // 2
    for at in range(0, rows, BIG):
        span = pl.ds(at, BIG)
        hat, _ = normed(tok[span, :].astype(F32))
        low = (hat * as_row(gain1) + as_row(shift1)).astype(BF16)
        queries[span, :] = dot(low, wq[...]).astype(BF16)
        logits[span, :] = dot_nt(low, router[...])
        both = dot(low, wkv[...])
        turned = pltpu.roll(both, LANES // 2, 1)
        kv[span, :LANES] = jnp.where(half_lane, both, turned).astype(BF16)
        kv[span, LANES:] = jnp.where(half_lane, turned, both).astype(BF16)
    for tile in range(tiles):
        at = tile * TILE
        span = pl.ds(at, TILE)
        meta = jnp.concatenate(
            [
                sent[:, at : at + TILE],
                valid[:, at : at + TILE],
                expert[:, at : at + TILE],
                jnp.zeros((4, TILE), jnp.int32),
            ],
            axis=0,
        ).astype(F32)
        column = jnp.transpose(meta)
        own_sent, own_valid = column[:, 0:1], column[:, 1:2]
        first_id, second_id = column[:, 2:3], column[:, 3:4]
        glow[span, :] = jnp.where(own_valid > 0.5, cot[span, :].astype(F32), 0.0).astype(BF16)
        scored = logits[span, :]
        slot = lax.broadcasted_iota(jnp.int32, scored.shape, 1).astype(F32)
        pick0 = jnp.sum(jnp.where(slot == first_id, scored, 0.0), axis=-1, keepdims=True)
        pick1 = jnp.sum(jnp.where(slot == second_id, scored, 0.0), axis=-1, keepdims=True)
        most = jnp.maximum(pick0, pick1)
        raise0, raise1 = jnp.exp(pick0 - most), jnp.exp(pick1 - most)
        gate0 = raise0 / (raise0 + raise1)
        gate1 = raise1 / (raise0 + raise1)
        lane = lax.broadcasted_iota(jnp.int32, (TILE, 8), 1)
        gates[span, :] = jnp.where(
            lane == 0, gate0, jnp.where(lane == 1, gate1, jnp.where(lane == 2, first_id, second_id))
        )
        masks = pair_masks(first_id, second_id, pairs)
        q0 = jnp.zeros((TILE, LANES), F32)
        q1 = jnp.zeros((TILE, LANES), F32)
        for pair in range(pairs):
            block = queries[span, pair * LANES : (pair + 1) * LANES].astype(F32)
            q0 = jnp.where(masks[pair][0], block, q0)
            q1 = jnp.where(masks[pair][1], block, q1)
        picked = (jnp.concatenate([q0, q1], axis=0) * scale).astype(BF16)
        qsel[tile] = picked
        start, extent = window_of(tile, tiles)
        near = pl.ds(start, extent)
        scores = dot_nt(picked, kv[near, :LANES])
        same = own_sent == sent[:, start : start + extent].astype(F32)
        same = jnp.concatenate([same, same], axis=0)
        scores = jnp.where(same, scores, -1e30)
        weights = jnp.exp(scores - jnp.max(scores, axis=-1, keepdims=True))
        share = (weights * (1.0 / jnp.sum(weights, axis=-1, keepdims=True))).astype(BF16)
        chance[tile] = share
        context = dot(share, kv[near, LANES:])
        part0 = context[:TILE] * gate0
        part1 = context[TILE:] * gate1
        for pair in range(pairs):
            mixed[span, pair * LANES : (pair + 1) * LANES] = jnp.where(
                masks[pair][0], part0, jnp.where(masks[pair][1], part1, 0.0)
            ).astype(BF16)
    for at in range(0, rows, BIG):
        span = pl.ds(at, BIG)
        total = tok[span, :].astype(F32) + dot(mixed[span, :], wo[...])
        res[span, :] = total.astype(BF16)
        hat, _ = normed(total)
        low2[span, :] = (hat * as_row(gain2) + as_row(shift2)).astype(BF16)


def ffn_kernel(*refs, units, more):
    low2, glow, weights = refs[:3]
    at = 3
    if "rows" in more:
        out_in, second_in = refs[at : at + 2]
        at += 2
    if "weights" in more:
        contract_in, expand_in, bias_in = refs[at : at + 3]
        at += 3
    if "final" in more:
        out, second, contract_out, folded_out, bias_out, hidden, grad = refs[at:]
    else:
        out, second, contract_out, expand_out, bias_out, hidden, grad = refs[at:]
    rows = low2.shape[0]
    contract = weights.at[:units, :]
    expand = weights.at[units + 16 :, :units]
    bias = weights[units : units + 1, :units].astype(F32)
    bias_sum = bias_in[...] if "weights" in more else jnp.zeros((1, units), F32)
    for first in range(0, rows, BIG):
        span = pl.ds(first, BIG)
        preact = dot(low2[span, :], expand[...]) + bias
        cumulative = 0.5 * (1.0 + lax.erf(preact * (1.0 / math.sqrt(2.0))))
        bell = jnp.exp(-0.5 * preact * preact) * (1.0 / math.sqrt(2.0 * math.pi))
        high = (preact * cumulative).astype(BF16)
        hidden[span, :] = high
        slope = cumulative + preact * bell
        low_grad = (dot_nt(glow[span, :], contract[...]) * slope).astype(BF16)
        grad[span, :] = low_grad
        bias_sum += row_sum(low_grad.astype(F32))
        out_part = dot(high, contract[...])
        second_part = dot_nt(low_grad, expand[...])
        if "rows" in more:
            out_part += out_in[span, :].astype(F32)
            second_part += second_in[span, :].astype(F32)
        out[span, :] = out_part.astype(out.dtype)
        second[span, :] = second_part.astype(second.dtype)
    contract_sum = dot_tn(hidden[...], glow[...])
    expand_sum = dot_tn(low2[...], grad[...])
    if "weights" in more:
        contract_sum += contract_in[...].astype(F32)
        expand_sum += expand_in[...].astype(F32)
    bias_out[...] = bias_sum
    if "final" in more:
        contract_out[...] = contract_sum.astype(contract_out.dtype)
        for at in range(0, expand_sum.shape[0], units):
            block = expand_sum[at : at + units, :]
            folded_out[:, at : at + units] = block.astype(folded_out.dtype)
    else:
        contract_out[...] = contract_sum.astype(contract_out.dtype)
        expand_out[...] = expand_sum.astype(expand_out.dtype)


def ffn(rows_far, low2, glow, weights, weights_far, units, rows_in=None, weights_in=None,
        rows_out=("far", "far"), final=False, carry="far"):
    rows, width = low2.shape
    more = []
    operands = [low2, glow, weights]
    spaces = [rows_far, rows_far, weights_far]
    if final:
        more.append("final")
    if rows_in is not None:
        more.append("rows")
        operands += rows_in
        spaces += ["far" if rows_far == "near" else "near"] * 2
    if weights_in is not None:
        more.append("weights")
        operands += weights_in
        spaces += [carry, carry, "near"]
    scratch = [pltpu.VMEM((rows, units), BF16), pltpu.VMEM((rows, units), BF16)]
    if final:
        sums = [jax.ShapeDtypeStruct((units, width), BF16)] * 2
    else:
        sums = [
            jax.ShapeDtypeStruct((units, width), BF16), jax.ShapeDtypeStruct((width, units), BF16)
        ]
    sums_out = [carry] * len(sums)
    outs = placed_call(
        functools.partial(ffn_kernel, units=units, more=tuple(more)),
        "ffn",
        operands,
        spaces,
        [jax.ShapeDtypeStruct((rows, width), BF16)] * 2
        + sums
        + [jax.ShapeDtypeStruct((1, units), F32)],
        list(rows_out) + sums_out + ["near"],
        scratch,
    )
    return list(outs[:2]), list(outs[2:])


def back_kernel(
    place, second_own, second_got, unit_own, unit_peers,
    res, glow, wo, gates, mixed, kv, chance, qsel, tok, wq, wkv,
    gain1, shift1, gain2, router,
    tok_grad, keep, send,
    packed, low1, grad_res, grad_mixed, grad_q, grad_log, key_sum, value_sum, vectors,
):
    rows, width = tok.shape
    tiles = rows // TILE
    pairs = width // LANES
    scale = (wkv.shape[1] // 2) ** -0.5
    experts = router.shape[0]
    gain_one, gain_two = as_row(gain1), as_row(gain2)
    gain2_sum = shift2_sum = bias_sum = jnp.zeros((1, width), F32)
    for at in range(0, rows, BIG):
        span = pl.ds(at, BIG)
        hat, inverse = normed(res[span, :].astype(F32))
        second = second_own[span, :].astype(F32) + second_got[span, :].astype(F32)
        gain2_sum += row_sum(second * hat)
        shift2_sum += row_sum(second)
        outer = glow[span, :].astype(F32)
        bias_sum += row_sum(outer)
        grad = outer + norm_back(second, gain_two, hat, inverse)
        grad_res[span, :] = grad
        grad_mixed[span, :] = dot_nt(grad.astype(BF16), wo[...])
    packed[:, width : 2 * width] = dot_tn(mixed[...], grad_res[...].astype(BF16)).astype(BF16)
    key_sum[...] = jnp.zeros_like(key_sum)
    value_sum[...] = jnp.zeros_like(value_sum)
    for tile in range(tiles):
        at = tile * TILE
        span = pl.ds(at, TILE)
        gate0, gate1 = gates[span, 0:1], gates[span, 1:2]
        first_id, second_id = gates[span, 2:3], gates[span, 3:4]
        masks = pair_masks(first_id, second_id, pairs)
        g0 = jnp.zeros((TILE, LANES), F32)
        g1 = jnp.zeros((TILE, LANES), F32)
        use0 = jnp.zeros((TILE, LANES), F32)
        use1 = jnp.zeros((TILE, LANES), F32)
        for pair in range(pairs):
            lanes = slice(pair * LANES, (pair + 1) * LANES)
            block = grad_mixed[span, lanes]
            both = block * mixed[span, lanes].astype(F32)
            g0 = jnp.where(masks[pair][0], block, g0)
            g1 = jnp.where(masks[pair][1], block, g1)
            use0 = jnp.where(masks[pair][0], both, use0)
            use1 = jnp.where(masks[pair][1], both, use1)
        use0 = jnp.sum(use0, axis=-1, keepdims=True)
        use1 = jnp.sum(use1, axis=-1, keepdims=True)
        turn = gate1 * use0 - gate0 * use1
        lane = lax.broadcasted_iota(jnp.int32, (TILE, LANES), 1).astype(F32)
        grad_log[span, :] = jnp.where(
            lane == first_id, turn, jnp.where(lane == second_id, -turn, 0.0)
        ).astype(BF16)
        grad_ctx = jnp.concatenate([g0 * gate0, g1 * gate1], axis=0).astype(BF16)
        delta = jnp.concatenate([use0, use1], axis=0)
        start, extent = window_of(tile, tiles)
        near = pl.ds(start, extent)
        grad_share = dot_nt(grad_ctx, kv[near, LANES:])
        share = chance[tile]
        raw = (share.astype(F32) * (grad_share - delta)).astype(BF16)
        grad_query = dot(raw, kv[near, :LANES]) * scale
        for pair in range(pairs):
            grad_q[span, pair * LANES : (pair + 1) * LANES] = jnp.where(
                masks[pair][0],
                grad_query[:TILE],
                jnp.where(masks[pair][1], grad_query[TILE:], 0.0),
            ).astype(BF16)
        key_sum[near, :] += dot_tn(raw, qsel[tile])
        value_sum[near, :] += dot_tn(share, grad_ctx)
    keys, values = key_sum[...], value_sum[...]
    keys = keys + pltpu.roll(keys, LANES // 2, 1)
    values = values + pltpu.roll(values, LANES // 2, 1)
    half_lane = lax.broadcasted_iota(jnp.int32, (rows, LANES), 1) < LANES // 2
    grad_kv = jnp.where(half_lane, keys, values).astype(BF16)
    gain1_sum = shift1_sum = jnp.zeros((1, width), F32)
    for at in range(0, rows, BIG):
        span = pl.ds(at, BIG)
        hat, inverse = normed(tok[span, :].astype(F32))
        low1[span, :] = (hat * gain_one + as_row(shift1)).astype(BF16)
        grad = (
            dot_nt(grad_q[span, :], wq[...])
            + dot_nt(grad_kv[at : at + BIG], wkv[...])
            + dot(grad_log[span, :experts], router[...])
        )
        gain1_sum += row_sum(grad * hat)
        shift1_sum += row_sum(grad)
        tok_grad[span, :] = (grad_res[span, :] + norm_back(grad, gain_one, hat, inverse)).astype(
            BF16
        )
    packed[:, :width] = dot_tn(low1[...], grad_q[...]).astype(BF16)
    packed[:, 2 * width : 2 * width + LANES] = dot_tn(low1[...], grad_kv).astype(BF16)
    vectors[...] = jnp.zeros_like(vectors)
    sums = (gain1_sum, shift1_sum, gain2_sum, shift2_sum, bias_sum)
    for at, values in enumerate(sums):
        vectors[VECTOR_ROW + at : VECTOR_ROW + at + 1, :] = values
    units = unit_own.shape[1]
    own = place[0]
    for step in range(unit_peers.shape[0] + 1):
        owner = own ^ (2 * step)
        part = unit_own[...] if step == 0 else unit_peers[step - 1 : step, :]
        vectors[pl.ds(VECTOR_ROW + len(sums) + owner, 1), :units] = part
    packed[:, 2 * width + LANES :] = (
        dot_tn(low1[...], grad_log[...]) + jnp.transpose(vectors[...])
    ).astype(BF16)
    half = width // 2
    mine = own % 2
    keep[...] = packed[pl.ds(pl.multiple_of(mine * half, half), half), :]
    send[...] = packed[pl.ds(pl.multiple_of((1 - mine) * half, half), half), :]


def unpack_kernel(
    place, mine, other,
    gain1, shift1, router, query, output, keyval, gain2, shift2, unit, bias,
    rest,
):
    half, width = mine.shape[0], query.shape[1]
    for end, values in ((place[0] % 2, mine), (1 - place[0] % 2, other)):
        span = pl.ds(pl.multiple_of(end * half, half), half)
        query[span, :] = values[:, :width].astype(F32)
        output[span, :] = values[:, width : 2 * width].astype(F32)
        keyval[span, :] = values[:, 2 * width : 2 * width + LANES].astype(F32)
        rest[span, :] = values[:, 2 * width + LANES :].astype(F32)
    rows = jnp.transpose(rest[...])
    router[...] = rows[: router.shape[0], :]
    for at, target in enumerate((gain1, shift1, gain2, shift2, bias)):
        target[...] = rows[VECTOR_ROW + at : VECTOR_ROW + at + 1, :]
    owner = lax.broadcasted_iota(jnp.int32, rows.shape, 0) - (VECTOR_ROW + 5)
    unit[...] = jnp.sum(jnp.where(owner == place[0], rows, 0.0), axis=0, keepdims=True)[
        :, : unit.shape[1]
    ]


def placed_call(kernel, name, operands, spaces, out_shape, out_spaces, scratch):
    where = {"far": pltpu.HBM, "near": pltpu.VMEM}
    lies = [pltpu.SMEM if space == "scalar" else pltpu.VMEM for space in spaces]
    operands = [
        pltpu.with_memory_space_constraint(item, where[space]) if space in where else item
        for item, space in zip(operands, spaces)
    ]
    results = [
        where[space](item.shape, item.dtype) if space in where else item
        for item, space in zip(out_shape, out_spaces)
    ]
    return pl.pallas_call(
        kernel,
        out_shape=results,
        in_specs=[pl.BlockSpec(memory_space=space) for space in lies],
        out_specs=[pl.BlockSpec(memory_space=pltpu.VMEM)] * len(results),
        scratch_shapes=scratch,
        compiler_params=pltpu.CompilerParams(vmem_limit_bytes=VMEM_LIMIT),
        cost_estimate=pl.CostEstimate(flops=1000, bytes_accessed=1000, transcendentals=0),
        name=name,
    )(*operands)


def swap(values, bit, devices):
    return lax.ppermute(values, AXES, [(at, at ^ bit) for at in range(devices)])


def halves(values, mine):
    size = values.shape[0] // 2
    keep = lax.dynamic_slice_in_dim(values, mine * size, size, 0)
    send = lax.dynamic_slice_in_dim(values, (1 - mine) * size, size, 0)
    return keep, send


def add_low(left, right):
    return (left.astype(F32) + right.astype(F32)).astype(BF16)


class Chain:
    def __init__(self, steps, place, devices):
        self.steps = list(steps)
        self.place, self.devices = place, devices
        self.values = self.keep = self.outgoing = None

    def mine(self, at):
        return (self.place // self.steps[at][1]) % 2

    def feed(self, values):
        self.values = values
        if self.steps and self.steps[0][0] == "cut":
            self.keep, self.outgoing = halves(values, self.mine(0))
        else:
            self.outgoing = values
        return self

    def feed_halves(self, keep, send):
        self.keep, self.outgoing = keep, send
        return self

    def send(self):
        return swap(self.outgoing, self.steps[0][1], self.devices)

    def take(self, got):
        kind = self.steps[0][0]
        if kind == "cut" and len(self.steps) > 1 and self.steps[1][0] == "cut":
            (keep, send), (keep_got, send_got) = (
                halves(item, self.mine(1)) for item in (self.keep, got)
            )
            self.outgoing = add_low(send, send_got)
            self.keep = add_low(keep, keep_got)
        else:
            if kind == "cut":
                values = add_low(self.keep, got)
            elif kind == "full":
                values = add_low(self.values, got)
            else:
                values = joined(self.values, got, self.mine(0))
            self.values = self.outgoing = values
        self.steps.pop(0)

    def run(self, steps):
        for _ in range(min(steps, len(self.steps))):
            self.take(self.send())
        return self.values


def plan(bits, whole=1):
    cut, full = bits[: len(bits) - whole], bits[len(bits) - whole :]
    return (
        [("cut", bit) for bit in cut]
        + [("full", bit) for bit in full]
        + [("join", bit) for bit in reversed(cut)]
    )


def sum_low(parts):
    return functools.reduce(jnp.add, [part.astype(F32) for part in parts]).astype(BF16)


def joined(values, got, mine):
    return jnp.where(
        mine == 0,
        jnp.concatenate([values, got], axis=0),
        jnp.concatenate([got, values], axis=0),
    )


def shards(
    n_dp,
    n_mp,
    tokens,
    sentence_ids,
    validity,
    expert_ids,
    cotangent,
    first_gain,
    first_shift,
    router,
    query_weight,
    output_weight,
    keyval_weight,
    second_gain,
    second_shift,
    expand_weight,
    expand_bias,
    contract_weight,
    contract_bias,
):
    devices = n_dp * n_mp
    rows, width = tokens.shape
    units = expand_weight.shape[1]
    tiles = rows // TILE
    _, extent = window_of(0, tiles)
    place = lax.axis_index(AXES)
    mp_place = lax.axis_index("mp")

    def row(vector):
        return vector.reshape(1, -1)

    def shape(*dims, dtype=BF16):
        return jax.ShapeDtypeStruct(dims, dtype)

    bias_rows = jnp.pad(expand_bias[None], ((0, 15), (0, width - units)))
    wide_expand = jnp.pad(expand_weight, ((0, 0), (0, width - units)))
    own = jnp.concatenate([contract_weight, bias_rows, wide_expand], axis=0)
    turned_router = router.T
    chips = n_mp // 2
    others = [swap(own, 2 * step, devices) for step in range(1, chips)]
    operands = [
        row(sentence_ids), row(validity), expert_ids.T, first_gain, first_shift, second_gain,
        second_shift, turned_router, tokens, query_weight, keyval_weight, cotangent, output_weight,
    ]
    res, low2, glow, mixed, qsel, kv, chance, gates = placed_call(
        attend_kernel,
        "attend",
        operands,
        ["far"] * len(operands),
        [shape(rows, width)] * 4
        + [
            shape(tiles, 2 * TILE, LANES),
            shape(rows, 2 * LANES),
            shape(tiles, 2 * TILE, extent),
            shape(rows, 8, dtype=F32),
        ],
        ["far", "near", "near"] + ["far"] * 5,
        [pltpu.VMEM((rows, width), BF16), pltpu.VMEM((rows, router.shape[1]), F32)],
    )
    low2_pair = swap(low2, 1, devices)
    glow_pair = swap(glow, 1, devices)
    dp_bits = [n_mp << at for at in range(n_dp.bit_length() - 1)]
    mp_bits = [1 << at for at in range(n_mp.bit_length() - 1)]
    rows_own, grads_own = ffn("near", low2, glow, own, "far", units)
    rows_pair, grads_own = ffn(
        None, low2_pair, glow_pair, own, "far", units, weights_in=grads_own, rows_out=(None, None),
        final=True,
    )
    contract_sum, expand_sum, unit_own = grads_own
    unit_peers = []
    waiting = []
    for step in range(1, chips):
        final = step == chips - 1
        rows_pair, grads = ffn(
            None,
            low2_pair,
            glow_pair,
            others[step - 1],
            None,
            units,
            rows_in=rows_pair,
            rows_out=(None, None),
        )
        if final:
            out_got, second_got = (swap(item, 1, devices) for item in rows_pair)
        rows_own, grads = ffn(
            "near",
            low2,
            glow,
            others[step - 1],
            None,
            units,
            rows_in=rows_own,
            weights_in=grads,
            rows_out=("far", "near" if final else "far"),
            final=True,
        )
        unit_peers.append(grads[2])
        waiting.append([swap(item, 2 * step, devices) for item in grads[:2]])
    scalars = jnp.full((1,), mp_place, jnp.int32)
    tok_grad, keep, send = placed_call(
        back_kernel,
        "back",
        [
            scalars, rows_own[1], second_got, unit_own, jnp.concatenate(unit_peers, axis=0),
            res, glow, output_weight, gates, mixed, kv, chance, qsel, tokens, query_weight,
            keyval_weight, first_gain, first_shift, second_gain, turned_router,
        ],
        ["scalar", "near", None, None, None, "far", "near"] + ["far"] * 13,
        [shape(rows, width)] + [shape(width // 2, 2 * width + 2 * LANES)] * 2,
        ["far", "near", "near"],
        [
            pltpu.VMEM((width, 2 * width + 2 * LANES), BF16),
            pltpu.VMEM((rows, width), BF16),
            pltpu.VMEM((rows, width), F32),
            pltpu.VMEM((rows, width), F32),
            pltpu.VMEM((rows, width), BF16),
            pltpu.VMEM((rows, LANES), BF16),
            pltpu.VMEM((rows, LANES), F32),
            pltpu.VMEM((rows, LANES), F32),
            pltpu.VMEM((LANES, width), F32),
        ],
    )
    order = mp_bits[:1] + dp_bits[:1] + mp_bits[1:] + dp_bits[1:]
    contract_got = [item[0] for item in waiting]
    expand_got = [item[1] for item in waiting]
    send, contract_got = lax.optimization_barrier((send, contract_got))
    first = Chain(plan(dp_bits[1:2] + dp_bits[:1] + dp_bits[2:], 1), place, devices)
    first.feed(sum_low([contract_sum, *contract_got]))
    second = Chain(plan(dp_bits, 1), place, devices)
    chain = Chain(plan(order, 1)[:-1], place, devices).feed_halves(keep, send)
    for at in range(len(chain.steps)):
        got = chain.send()
        if at == 1:
            got, expand_got = lax.optimization_barrier((got, expand_got))
            second.feed(sum_low([expand_sum, *expand_got]))
        chain.take(got)
    packed = chain.values
    layer = (
        res.astype(F32) + rows_own[0].astype(F32) + out_got.astype(F32) + contract_bias.astype(F32)
    ).astype(BF16)
    contract_sum = first.run(len(first.steps))
    contract_grad = contract_sum.astype(F32)
    other = swap(packed, mp_bits[0], devices)
    square = shape(width, width, dtype=F32)
    line = shape(1, width, dtype=F32)
    unpacked = placed_call(
        unpack_kernel,
        "unpack",
        [scalars, packed, other],
        ["scalar", None, None],
        [
            line, line, shape(router.shape[1], width, dtype=F32), square, square,
            shape(width, LANES, dtype=F32), line, line, shape(1, units, dtype=F32), line,
        ],
        [None] * 10,
        [pltpu.VMEM((width, LANES), F32)],
    )
    second.run(len(second.steps) - 1)
    got, unpacked, layer = lax.optimization_barrier((second.send(), unpacked, layer))
    second.take(got)
    expand_sum = second.values
    expand_grad = jnp.concatenate(
        [expand_sum[:, at : at + units] for at in range(0, width, units)], axis=0
    ).astype(F32)
    (
        gain1_grad, shift1_grad, router_grad, query_grad, output_grad, keyval_grad, gain2_grad,
        shift2_grad, unit_grad, bias_grad,
    ) = unpacked
    return (
        layer,
        tok_grad,
        gain1_grad[0],
        shift1_grad[0],
        router_grad.T,
        query_grad,
        output_grad,
        keyval_grad,
        gain2_grad[0],
        shift2_grad[0],
        expand_grad,
        unit_grad[0],
        contract_grad,
        bias_grad[0],
    )


def solution(mesh):
    tokens_spec = P(AXES, None)
    placed = (
        tokens_spec,
        P(AXES),
        P(AXES),
        tokens_spec,
        tokens_spec,
        P(),
        P(),
        P(),
        P(),
        P(),
        P(),
        P(),
        P(),
        P(None, "mp"),
        P("mp"),
        P("mp", None),
        P(),
    )
    return jax.shard_map(
        functools.partial(shards, mesh.shape["dp"], mesh.shape["mp"]),
        mesh=mesh,
        in_specs=placed,
        out_specs=(
            tokens_spec,
            tokens_spec,
            P(),
            P(),
            P(),
            P(),
            P(),
            P(),
            P(),
            P(),
            P(None, "mp"),
            P("mp"),
            P("mp", None),
            P(),
        ),
        check_vma=False,
    )
```

```python
import functools
import math

import jax
import jax.numpy as jnp
from jax import lax
from jax.experimental import pallas as pl
from jax.experimental.pallas import tpu as pltpu
from jax.sharding import PartitionSpec as P

F32 = jnp.float32
BF16 = jnp.bfloat16
epsilon = 1e-05
AXES = ("dp", "mp")
TILE = 128
BIG = 512
VMEM_LIMIT = 36 << 20
LANES = 128
VECTOR_ROW = 8


def dot(left, right):
    return lax.dot_general(left, right, (((1,), (0,)), ((), ())), preferred_element_type=F32)


def dot_nt(left, right):
    return lax.dot_general(left, right, (((1,), (1,)), ((), ())), preferred_element_type=F32)


def dot_tn(left, right):
    return lax.dot_general(left, right, (((0,), (0,)), ((), ())), preferred_element_type=F32)


def normed(rows_in):
    middle = jnp.mean(rows_in, axis=-1, keepdims=True)
    center = rows_in - middle
    inverse = lax.rsqrt(jnp.mean(center * center, axis=-1, keepdims=True) + epsilon)
    return center * inverse, inverse


def norm_back(grad_normed, gain, normed_hat, inverse):
    scaled = grad_normed * gain
    mean_one = jnp.mean(scaled, axis=-1, keepdims=True)
    mean_two = jnp.mean(scaled * normed_hat, axis=-1, keepdims=True)
    return inverse * (scaled - mean_one - normed_hat * mean_two)


def as_row(vector):
    return vector[...].astype(F32).reshape(1, -1)


def row_sum(values):
    return jnp.sum(values, axis=0, keepdims=True)


def pair_masks(first_id, second_id, pairs):
    half = (lax.broadcasted_iota(jnp.int32, (TILE, LANES), 1) >= LANES // 2).astype(F32)
    low = first_id - half
    high = second_id - half
    return [(low == 2.0 * pair, high == 2.0 * pair) for pair in range(pairs)]


def window_of(tile, tiles):
    width = min(3, tiles)
    return min(max(tile - 1, 0), tiles - width) * TILE, width * TILE


def attend_kernel(
    sent, valid, expert, gain1, shift1, gain2, shift2, router, tok, wq, wkv, cot, wo,
    res, low2, glow, mixed, qsel, kv, chance, gates,
    queries, logits,
):
    rows, width = tok.shape
    tiles = rows // TILE
    pairs = width // LANES
    scale = (wkv.shape[1] // 2) ** -0.5
    half_lane = lax.broadcasted_iota(jnp.int32, (BIG, LANES), 1) < LANES // 2
    for at in range(0, rows, BIG):
        span = pl.ds(at, BIG)
        hat, _ = normed(tok[span, :].astype(F32))
        low = (hat * as_row(gain1) + as_row(shift1)).astype(BF16)
        queries[span, :] = dot(low, wq[...]).astype(BF16)
        logits[span, :] = dot_nt(low, router[...])
        both = dot(low, wkv[...])
        turned = pltpu.roll(both, LANES // 2, 1)
        kv[span, :LANES] = jnp.where(half_lane, both, turned).astype(BF16)
        kv[span, LANES:] = jnp.where(half_lane, turned, both).astype(BF16)
    for tile in range(tiles):
        at = tile * TILE
        span = pl.ds(at, TILE)
        meta = jnp.concatenate(
            [
                sent[:, at : at + TILE],
                valid[:, at : at + TILE],
                expert[:, at : at + TILE],
                jnp.zeros((4, TILE), jnp.int32),
            ],
            axis=0,
        ).astype(F32)
        column = jnp.transpose(meta)
        own_sent, own_valid = column[:, 0:1], column[:, 1:2]
        first_id, second_id = column[:, 2:3], column[:, 3:4]
        glow[span, :] = jnp.where(own_valid > 0.5, cot[span, :].astype(F32), 0.0).astype(BF16)
        scored = logits[span, :]
        slot = lax.broadcasted_iota(jnp.int32, scored.shape, 1).astype(F32)
        pick0 = jnp.sum(jnp.where(slot == first_id, scored, 0.0), axis=-1, keepdims=True)
        pick1 = jnp.sum(jnp.where(slot == second_id, scored, 0.0), axis=-1, keepdims=True)
        most = jnp.maximum(pick0, pick1)
        raise0, raise1 = jnp.exp(pick0 - most), jnp.exp(pick1 - most)
        gate0 = raise0 / (raise0 + raise1)
        gate1 = raise1 / (raise0 + raise1)
        lane = lax.broadcasted_iota(jnp.int32, (TILE, 8), 1)
        gates[span, :] = jnp.where(
            lane == 0, gate0, jnp.where(lane == 1, gate1, jnp.where(lane == 2, first_id, second_id))
        )
        masks = pair_masks(first_id, second_id, pairs)
        q0 = jnp.zeros((TILE, LANES), F32)
        q1 = jnp.zeros((TILE, LANES), F32)
        for pair in range(pairs):
            block = queries[span, pair * LANES : (pair + 1) * LANES].astype(F32)
            q0 = jnp.where(masks[pair][0], block, q0)
            q1 = jnp.where(masks[pair][1], block, q1)
        picked = (jnp.concatenate([q0, q1], axis=0) * scale).astype(BF16)
        qsel[tile] = picked
        start, extent = window_of(tile, tiles)
        near = pl.ds(start, extent)
        scores = dot_nt(picked, kv[near, :LANES])
        same = own_sent == sent[:, start : start + extent].astype(F32)
        same = jnp.concatenate([same, same], axis=0)
        scores = jnp.where(same, scores, -1e30)
        weights = jnp.exp(scores - jnp.max(scores, axis=-1, keepdims=True))
        share = (weights * (1.0 / jnp.sum(weights, axis=-1, keepdims=True))).astype(BF16)
        chance[tile] = share
        context = dot(share, kv[near, LANES:])
        part0 = context[:TILE] * gate0
        part1 = context[TILE:] * gate1
        for pair in range(pairs):
            mixed[span, pair * LANES : (pair + 1) * LANES] = jnp.where(
                masks[pair][0], part0, jnp.where(masks[pair][1], part1, 0.0)
            ).astype(BF16)
    for at in range(0, rows, BIG):
        span = pl.ds(at, BIG)
        total = tok[span, :].astype(F32) + dot(mixed[span, :], wo[...])
        res[span, :] = total.astype(BF16)
        hat, _ = normed(total)
        low2[span, :] = (hat * as_row(gain2) + as_row(shift2)).astype(BF16)


def ffn_kernel(*refs, units, more):
    low2, glow, weights = refs[:3]
    at = 3
    if "rows" in more:
        out_in, second_in = refs[at : at + 2]
        at += 2
    if "weights" in more:
        contract_in, expand_in, bias_in = refs[at : at + 3]
        at += 3
    if "final" in more:
        out, second, contract_out, folded_out, bias_out, hidden, grad = refs[at:]
    else:
        out, second, contract_out, expand_out, bias_out, hidden, grad = refs[at:]
    rows = low2.shape[0]
    contract = weights.at[:units, :]
    expand = weights.at[units + 16 :, :units]
    bias = weights[units : units + 1, :units].astype(F32)
    bias_sum = bias_in[...] if "weights" in more else jnp.zeros((1, units), F32)
    for first in range(0, rows, BIG):
        span = pl.ds(first, BIG)
        preact = dot(low2[span, :], expand[...]) + bias
        cumulative = 0.5 * (1.0 + lax.erf(preact * (1.0 / math.sqrt(2.0))))
        bell = jnp.exp(-0.5 * preact * preact) * (1.0 / math.sqrt(2.0 * math.pi))
        high = (preact * cumulative).astype(BF16)
        hidden[span, :] = high
        slope = cumulative + preact * bell
        low_grad = (dot_nt(glow[span, :], contract[...]) * slope).astype(BF16)
        grad[span, :] = low_grad
        bias_sum += row_sum(low_grad.astype(F32))
        out_part = dot(high, contract[...])
        second_part = dot_nt(low_grad, expand[...])
        if "rows" in more:
            out_part += out_in[span, :].astype(F32)
            second_part += second_in[span, :].astype(F32)
        out[span, :] = out_part.astype(out.dtype)
        second[span, :] = second_part.astype(second.dtype)
    contract_sum = dot_tn(hidden[...], glow[...])
    expand_sum = dot_tn(low2[...], grad[...])
    if "weights" in more:
        contract_sum += contract_in[...].astype(F32)
        expand_sum += expand_in[...].astype(F32)
    bias_out[...] = bias_sum
    if "final" in more:
        contract_out[...] = contract_sum.astype(contract_out.dtype)
        for at in range(0, expand_sum.shape[0], units):
            block = expand_sum[at : at + units, :]
            folded_out[:, at : at + units] = block.astype(folded_out.dtype)
    else:
        contract_out[...] = contract_sum.astype(contract_out.dtype)
        expand_out[...] = expand_sum.astype(expand_out.dtype)


def ffn(rows_far, low2, glow, weights, weights_far, units, rows_in=None, weights_in=None,
        rows_out=("far", "far"), final=False, carry="far"):
    rows, width = low2.shape
    more = []
    operands = [low2, glow, weights]
    spaces = [rows_far, rows_far, weights_far]
    if final:
        more.append("final")
    if rows_in is not None:
        more.append("rows")
        operands += rows_in
        spaces += ["far" if rows_far == "near" else "near"] * 2
    if weights_in is not None:
        more.append("weights")
        operands += weights_in
        spaces += [carry, carry, "near"]
    scratch = [pltpu.VMEM((rows, units), BF16), pltpu.VMEM((rows, units), BF16)]
    if final:
        sums = [jax.ShapeDtypeStruct((units, width), BF16)] * 2
    else:
        sums = [
            jax.ShapeDtypeStruct((units, width), BF16), jax.ShapeDtypeStruct((width, units), BF16)
        ]
    sums_out = [carry] * len(sums)
    outs = placed_call(
        functools.partial(ffn_kernel, units=units, more=tuple(more)),
        "ffn",
        operands,
        spaces,
        [jax.ShapeDtypeStruct((rows, width), BF16)] * 2
        + sums
        + [jax.ShapeDtypeStruct((1, units), F32)],
        list(rows_out) + sums_out + ["near"],
        scratch,
    )
    return list(outs[:2]), list(outs[2:])


def back_kernel(
    place, second_own, second_got, unit_own, unit_peers,
    res, glow, wo, gates, mixed, kv, chance, qsel, tok, wq, wkv,
    gain1, shift1, gain2, router,
    tok_grad, keep, send,
    packed, low1, grad_res, grad_mixed, grad_q, grad_log, key_sum, value_sum, vectors,
):
    rows, width = tok.shape
    tiles = rows // TILE
    pairs = width // LANES
    scale = (wkv.shape[1] // 2) ** -0.5
    experts = router.shape[0]
    gain_one, gain_two = as_row(gain1), as_row(gain2)
    gain2_sum = shift2_sum = bias_sum = jnp.zeros((1, width), F32)
    for at in range(0, rows, BIG):
        span = pl.ds(at, BIG)
        hat, inverse = normed(res[span, :].astype(F32))
        second = second_own[span, :].astype(F32) + second_got[span, :].astype(F32)
        gain2_sum += row_sum(second * hat)
        shift2_sum += row_sum(second)
        outer = glow[span, :].astype(F32)
        bias_sum += row_sum(outer)
        grad = outer + norm_back(second, gain_two, hat, inverse)
        grad_res[span, :] = grad
        grad_mixed[span, :] = dot_nt(grad.astype(BF16), wo[...])
    packed[:, width : 2 * width] = dot_tn(mixed[...], grad_res[...].astype(BF16)).astype(BF16)
    key_sum[...] = jnp.zeros_like(key_sum)
    value_sum[...] = jnp.zeros_like(value_sum)
    for tile in range(tiles):
        at = tile * TILE
        span = pl.ds(at, TILE)
        gate0, gate1 = gates[span, 0:1], gates[span, 1:2]
        first_id, second_id = gates[span, 2:3], gates[span, 3:4]
        masks = pair_masks(first_id, second_id, pairs)
        g0 = jnp.zeros((TILE, LANES), F32)
        g1 = jnp.zeros((TILE, LANES), F32)
        use0 = jnp.zeros((TILE, LANES), F32)
        use1 = jnp.zeros((TILE, LANES), F32)
        for pair in range(pairs):
            lanes = slice(pair * LANES, (pair + 1) * LANES)
            block = grad_mixed[span, lanes]
            both = block * mixed[span, lanes].astype(F32)
            g0 = jnp.where(masks[pair][0], block, g0)
            g1 = jnp.where(masks[pair][1], block, g1)
            use0 = jnp.where(masks[pair][0], both, use0)
            use1 = jnp.where(masks[pair][1], both, use1)
        use0 = jnp.sum(use0, axis=-1, keepdims=True)
        use1 = jnp.sum(use1, axis=-1, keepdims=True)
        turn = gate1 * use0 - gate0 * use1
        lane = lax.broadcasted_iota(jnp.int32, (TILE, LANES), 1).astype(F32)
        grad_log[span, :] = jnp.where(
            lane == first_id, turn, jnp.where(lane == second_id, -turn, 0.0)
        ).astype(BF16)
        grad_ctx = jnp.concatenate([g0 * gate0, g1 * gate1], axis=0).astype(BF16)
        delta = jnp.concatenate([use0, use1], axis=0)
        start, extent = window_of(tile, tiles)
        near = pl.ds(start, extent)
        grad_share = dot_nt(grad_ctx, kv[near, LANES:])
        share = chance[tile]
        raw = (share.astype(F32) * (grad_share - delta)).astype(BF16)
        grad_query = dot(raw, kv[near, :LANES]) * scale
        for pair in range(pairs):
            grad_q[span, pair * LANES : (pair + 1) * LANES] = jnp.where(
                masks[pair][0],
                grad_query[:TILE],
                jnp.where(masks[pair][1], grad_query[TILE:], 0.0),
            ).astype(BF16)
        key_sum[near, :] += dot_tn(raw, qsel[tile])
        value_sum[near, :] += dot_tn(share, grad_ctx)
    keys, values = key_sum[...], value_sum[...]
    keys = keys + pltpu.roll(keys, LANES // 2, 1)
    values = values + pltpu.roll(values, LANES // 2, 1)
    half_lane = lax.broadcasted_iota(jnp.int32, (rows, LANES), 1) < LANES // 2
    grad_kv = jnp.where(half_lane, keys, values).astype(BF16)
    gain1_sum = shift1_sum = jnp.zeros((1, width), F32)
    for at in range(0, rows, BIG):
        span = pl.ds(at, BIG)
        hat, inverse = normed(tok[span, :].astype(F32))
        low1[span, :] = (hat * gain_one + as_row(shift1)).astype(BF16)
        grad = (
            dot_nt(grad_q[span, :], wq[...])
            + dot_nt(grad_kv[at : at + BIG], wkv[...])
            + dot(grad_log[span, :experts], router[...])
        )
        gain1_sum += row_sum(grad * hat)
        shift1_sum += row_sum(grad)
        tok_grad[span, :] = (grad_res[span, :] + norm_back(grad, gain_one, hat, inverse)).astype(
            BF16
        )
    packed[:, :width] = dot_tn(low1[...], grad_q[...]).astype(BF16)
    packed[:, 2 * width : 2 * width + LANES] = dot_tn(low1[...], grad_kv).astype(BF16)
    vectors[...] = jnp.zeros_like(vectors)
    sums = (gain1_sum, shift1_sum, gain2_sum, shift2_sum, bias_sum)
    for at, values in enumerate(sums):
        vectors[VECTOR_ROW + at : VECTOR_ROW + at + 1, :] = values
    units = unit_own.shape[1]
    own = place[0]
    for step in range(unit_peers.shape[0] + 1):
        owner = own ^ (2 * step)
        part = unit_own[...] if step == 0 else unit_peers[step - 1 : step, :]
        vectors[pl.ds(VECTOR_ROW + len(sums) + owner, 1), :units] = part
    packed[:, 2 * width + LANES :] = (
        dot_tn(low1[...], grad_log[...]) + jnp.transpose(vectors[...])
    ).astype(BF16)
    half = width // 2
    mine = own % 2
    keep[...] = packed[pl.ds(pl.multiple_of(mine * half, half), half), :]
    send[...] = packed[pl.ds(pl.multiple_of((1 - mine) * half, half), half), :]


def unpack_kernel(
    place, mine, other,
    gain1, shift1, router, query, output, keyval, gain2, shift2, unit, bias,
    rest,
):
    half, width = mine.shape[0], query.shape[1]
    for end, values in ((place[0] % 2, mine), (1 - place[0] % 2, other)):
        span = pl.ds(pl.multiple_of(end * half, half), half)
        query[span, :] = values[:, :width].astype(F32)
        output[span, :] = values[:, width : 2 * width].astype(F32)
        keyval[span, :] = values[:, 2 * width : 2 * width + LANES].astype(F32)
        rest[span, :] = values[:, 2 * width + LANES :].astype(F32)
    rows = jnp.transpose(rest[...])
    router[...] = rows[: router.shape[0], :]
    for at, target in enumerate((gain1, shift1, gain2, shift2, bias)):
        target[...] = rows[VECTOR_ROW + at : VECTOR_ROW + at + 1, :]
    owner = lax.broadcasted_iota(jnp.int32, rows.shape, 0) - (VECTOR_ROW + 5)
    unit[...] = jnp.sum(jnp.where(owner == place[0], rows, 0.0), axis=0, keepdims=True)[
        :, : unit.shape[1]
    ]


def placed_call(kernel, name, operands, spaces, out_shape, out_spaces, scratch):
    where = {"far": pltpu.HBM, "near": pltpu.VMEM}
    lies = [pltpu.SMEM if space == "scalar" else pltpu.VMEM for space in spaces]
    operands = [
        pltpu.with_memory_space_constraint(item, where[space]) if space in where else item
        for item, space in zip(operands, spaces)
    ]
    results = [
        where[space](item.shape, item.dtype) if space in where else item
        for item, space in zip(out_shape, out_spaces)
    ]
    return pl.pallas_call(
        kernel,
        out_shape=results,
        in_specs=[pl.BlockSpec(memory_space=space) for space in lies],
        out_specs=[pl.BlockSpec(memory_space=pltpu.VMEM)] * len(results),
        scratch_shapes=scratch,
        compiler_params=pltpu.CompilerParams(vmem_limit_bytes=VMEM_LIMIT),
        cost_estimate=pl.CostEstimate(flops=1000, bytes_accessed=1000, transcendentals=0),
        name=name,
    )(*operands)


def swap(values, bit, devices):
    return lax.ppermute(values, AXES, [(at, at ^ bit) for at in range(devices)])


def halves(values, mine):
    size = values.shape[0] // 2
    keep = lax.dynamic_slice_in_dim(values, mine * size, size, 0)
    send = lax.dynamic_slice_in_dim(values, (1 - mine) * size, size, 0)
    return keep, send


def add_low(left, right):
    return (left.astype(F32) + right.astype(F32)).astype(BF16)


class Chain:
    def __init__(self, steps, place, devices):
        self.steps = list(steps)
        self.place, self.devices = place, devices
        self.values = self.keep = self.outgoing = None

    def mine(self, at):
        return (self.place // self.steps[at][1]) % 2

    def feed(self, values):
        self.values = values
        if self.steps and self.steps[0][0] == "cut":
            self.keep, self.outgoing = halves(values, self.mine(0))
        else:
            self.outgoing = values
        return self

    def feed_halves(self, keep, send):
        self.keep, self.outgoing = keep, send
        return self

    def send(self):
        return swap(self.outgoing, self.steps[0][1], self.devices)

    def take(self, got):
        kind = self.steps[0][0]
        if kind == "cut" and len(self.steps) > 1 and self.steps[1][0] == "cut":
            (keep, send), (keep_got, send_got) = (
                halves(item, self.mine(1)) for item in (self.keep, got)
            )
            self.outgoing = add_low(send, send_got)
            self.keep = add_low(keep, keep_got)
        else:
            if kind == "cut":
                values = add_low(self.keep, got)
            elif kind == "full":
                values = add_low(self.values, got)
            else:
                values = joined(self.values, got, self.mine(0))
            self.values = self.outgoing = values
        self.steps.pop(0)

    def run(self, steps):
        for _ in range(min(steps, len(self.steps))):
            self.take(self.send())
        return self.values


def plan(bits, whole=1):
    cut, full = bits[: len(bits) - whole], bits[len(bits) - whole :]
    return (
        [("cut", bit) for bit in cut]
        + [("full", bit) for bit in full]
        + [("join", bit) for bit in reversed(cut)]
    )


def sum_low(parts):
    return functools.reduce(jnp.add, [part.astype(F32) for part in parts]).astype(BF16)


def joined(values, got, mine):
    return jnp.where(
        mine == 0,
        jnp.concatenate([values, got], axis=0),
        jnp.concatenate([got, values], axis=0),
    )


def shards(
    n_dp,
    n_mp,
    tokens,
    sentence_ids,
    validity,
    expert_ids,
    cotangent,
    first_gain,
    first_shift,
    router,
    query_weight,
    output_weight,
    keyval_weight,
    second_gain,
    second_shift,
    expand_weight,
    expand_bias,
    contract_weight,
    contract_bias,
):
    devices = n_dp * n_mp
    rows, width = tokens.shape
    units = expand_weight.shape[1]
    tiles = rows // TILE
    _, extent = window_of(0, tiles)
    place = lax.axis_index(AXES)
    mp_place = lax.axis_index("mp")

    def row(vector):
        return vector.reshape(1, -1)

    def shape(*dims, dtype=BF16):
        return jax.ShapeDtypeStruct(dims, dtype)

    bias_rows = jnp.pad(expand_bias[None], ((0, 15), (0, width - units)))
    wide_expand = jnp.pad(expand_weight, ((0, 0), (0, width - units)))
    own = jnp.concatenate([contract_weight, bias_rows, wide_expand], axis=0)
    turned_router = router.T
    chips = n_mp // 2
    others = [swap(own, 2 * step, devices) for step in range(1, chips)]
    operands = [
        row(sentence_ids), row(validity), expert_ids.T, first_gain, first_shift, second_gain,
        second_shift, turned_router, tokens, query_weight, keyval_weight, cotangent, output_weight,
    ]
    res, low2, glow, mixed, qsel, kv, chance, gates = placed_call(
        attend_kernel,
        "attend",
        operands,
        ["far"] * len(operands),
        [shape(rows, width)] * 4
        + [
            shape(tiles, 2 * TILE, LANES),
            shape(rows, 2 * LANES),
            shape(tiles, 2 * TILE, extent),
            shape(rows, 8, dtype=F32),
        ],
        ["far", "near", "near"] + ["far"] * 5,
        [pltpu.VMEM((rows, width), BF16), pltpu.VMEM((rows, router.shape[1]), F32)],
    )
    low2_pair = swap(low2, 1, devices)
    glow_pair = swap(glow, 1, devices)
    dp_bits = [n_mp << at for at in range(n_dp.bit_length() - 1)]
    mp_bits = [1 << at for at in range(n_mp.bit_length() - 1)]
    rows_own, grads_own = ffn("near", low2, glow, own, "far", units)
    rows_pair, grads_own = ffn(
        None, low2_pair, glow_pair, own, "far", units, weights_in=grads_own, rows_out=(None, None),
        final=True,
    )
    contract_sum, expand_sum, unit_own = grads_own
    unit_peers = []
    waiting = []
    for step in range(1, chips):
        final = step == chips - 1
        rows_pair, grads = ffn(
            None,
            low2_pair,
            glow_pair,
            others[step - 1],
            None,
            units,
            rows_in=rows_pair,
            rows_out=(None, None),
        )
        if final:
            out_got, second_got = (swap(item, 1, devices) for item in rows_pair)
        rows_own, grads = ffn(
            "near",
            low2,
            glow,
            others[step - 1],
            None,
            units,
            rows_in=rows_own,
            weights_in=grads,
            rows_out=("far", "near" if final else "far"),
            final=True,
        )
        unit_peers.append(grads[2])
        waiting.append([swap(item, 2 * step, devices) for item in grads[:2]])
    scalars = jnp.full((1,), mp_place, jnp.int32)
    tok_grad, keep, send = placed_call(
        back_kernel,
        "back",
        [
            scalars, rows_own[1], second_got, unit_own, jnp.concatenate(unit_peers, axis=0),
            res, glow, output_weight, gates, mixed, kv, chance, qsel, tokens, query_weight,
            keyval_weight, first_gain, first_shift, second_gain, turned_router,
        ],
        ["scalar", "near", None, None, None, "far", "near"] + ["far"] * 13,
        [shape(rows, width)] + [shape(width // 2, 2 * width + 2 * LANES)] * 2,
        ["far", "near", "near"],
        [
            pltpu.VMEM((width, 2 * width + 2 * LANES), BF16),
            pltpu.VMEM((rows, width), BF16),
            pltpu.VMEM((rows, width), F32),
            pltpu.VMEM((rows, width), F32),
            pltpu.VMEM((rows, width), BF16),
            pltpu.VMEM((rows, LANES), BF16),
            pltpu.VMEM((rows, LANES), F32),
            pltpu.VMEM((rows, LANES), F32),
            pltpu.VMEM((LANES, width), F32),
        ],
    )
    order = mp_bits[:1] + dp_bits[:1] + mp_bits[1:] + dp_bits[1:]
    contract_got = [item[0] for item in waiting]
    expand_got = [item[1] for item in waiting]
    send, contract_got = lax.optimization_barrier((send, contract_got))
    first = Chain(plan(dp_bits[1:2] + dp_bits[:1] + dp_bits[2:], 1), place, devices)
    first.feed(sum_low([contract_sum, *contract_got]))
    second = Chain(plan(dp_bits, 1), place, devices)
    chain = Chain(plan(order, 1)[:-1], place, devices).feed_halves(keep, send)
    for at in range(len(chain.steps)):
        got = chain.send()
        if at == 1:
            got, expand_got = lax.optimization_barrier((got, expand_got))
            second.feed(sum_low([expand_sum, *expand_got]))
        chain.take(got)
    packed = chain.values
    layer = (
        res.astype(F32) + rows_own[0].astype(F32) + out_got.astype(F32) + contract_bias.astype(F32)
    ).astype(BF16)
    contract_sum = first.run(len(first.steps))
    contract_grad = contract_sum.astype(F32)
    other = swap(packed, mp_bits[0], devices)
    square = shape(width, width, dtype=F32)
    line = shape(1, width, dtype=F32)
    unpacked = placed_call(
        unpack_kernel,
        "unpack",
        [scalars, packed, other],
        ["scalar", None, None],
        [
            line, line, shape(router.shape[1], width, dtype=F32), square, square,
            shape(width, LANES, dtype=F32), line, line, shape(1, units, dtype=F32), line,
        ],
        [None] * 10,
        [pltpu.VMEM((width, LANES), F32)],
    )
    second.run(len(second.steps) - 1)
    got, unpacked, layer = lax.optimization_barrier((second.send(), unpacked, layer))
    second.take(got)
    expand_sum = second.values
    expand_grad = jnp.concatenate(
        [expand_sum[:, at : at + units] for at in range(0, width, units)], axis=0
    ).astype(F32)
    (
        gain1_grad, shift1_grad, router_grad, query_grad, output_grad, keyval_grad, gain2_grad,
        shift2_grad, unit_grad, bias_grad,
    ) = unpacked
    return (
        layer,
        tok_grad,
        gain1_grad[0],
        shift1_grad[0],
        router_grad.T,
        query_grad,
        output_grad,
        keyval_grad,
        gain2_grad[0],
        shift2_grad[0],
        expand_grad,
        unit_grad[0],
        contract_grad,
        bias_grad[0],
    )


def solution(mesh):
    tokens_spec = P(AXES, None)
    placed = (
        tokens_spec,
        P(AXES),
        P(AXES),
        tokens_spec,
        tokens_spec,
        P(),
        P(),
        P(),
        P(),
        P(),
        P(),
        P(),
        P(),
        P(None, "mp"),
        P("mp"),
        P("mp", None),
        P(),
    )
    return jax.shard_map(
        functools.partial(shards, mesh.shape["dp"], mesh.shape["mp"]),
        mesh=mesh,
        in_specs=placed,
        out_specs=(
            tokens_spec,
            tokens_spec,
            P(),
            P(),
            P(),
            P(),
            P(),
            P(),
            P(),
            P(),
            P(None, "mp"),
            P("mp"),
            P("mp", None),
            P(),
        ),
        check_vma=False,
    )
```

```python
import functools
import math

import jax
import jax.numpy as jnp
from jax import lax
from jax.experimental import pallas as pl
from jax.experimental.pallas import tpu as pltpu
from jax.sharding import PartitionSpec as P

F32 = jnp.float32
BF16 = jnp.bfloat16
epsilon = 1e-05
AXES = ("dp", "mp")
TILE = 128
BIG = 512
VMEM_LIMIT = 36 << 20
LANES = 128
VECTOR_ROW = 8


def dot(left, right):
    return lax.dot_general(left, right, (((1,), (0,)), ((), ())), preferred_element_type=F32)


def dot_nt(left, right):
    return lax.dot_general(left, right, (((1,), (1,)), ((), ())), preferred_element_type=F32)


def dot_tn(left, right):
    return lax.dot_general(left, right, (((0,), (0,)), ((), ())), preferred_element_type=F32)


def normed(rows_in):
    middle = jnp.mean(rows_in, axis=-1, keepdims=True)
    center = rows_in - middle
    inverse = lax.rsqrt(jnp.mean(center * center, axis=-1, keepdims=True) + epsilon)
    return center * inverse, inverse


def norm_back(grad_normed, gain, normed_hat, inverse):
    scaled = grad_normed * gain
    mean_one = jnp.mean(scaled, axis=-1, keepdims=True)
    mean_two = jnp.mean(scaled * normed_hat, axis=-1, keepdims=True)
    return inverse * (scaled - mean_one - normed_hat * mean_two)


def as_row(vector):
    return vector[...].astype(F32).reshape(1, -1)


def row_sum(values):
    return jnp.sum(values, axis=0, keepdims=True)


def pair_masks(first_id, second_id, pairs):
    half = (lax.broadcasted_iota(jnp.int32, (TILE, LANES), 1) >= LANES // 2).astype(F32)
    low = first_id - half
    high = second_id - half
    return [(low == 2.0 * pair, high == 2.0 * pair) for pair in range(pairs)]


def window_of(tile, tiles):
    width = min(3, tiles)
    return min(max(tile - 1, 0), tiles - width) * TILE, width * TILE


def attend_kernel(
    sent, valid, expert, gain1, shift1, gain2, shift2, router, tok, wq, wkv, cot, wo,
    res, low2, glow, mixed, qsel, kv, chance, gates,
    queries, logits,
):
    rows, width = tok.shape
    tiles = rows // TILE
    pairs = width // LANES
    scale = (wkv.shape[1] // 2) ** -0.5
    half_lane = lax.broadcasted_iota(jnp.int32, (BIG, LANES), 1) < LANES // 2
    for at in range(0, rows, BIG):
        span = pl.ds(at, BIG)
        hat, _ = normed(tok[span, :].astype(F32))
        low = (hat * as_row(gain1) + as_row(shift1)).astype(BF16)
        queries[span, :] = dot(low, wq[...]).astype(BF16)
        logits[span, :] = dot_nt(low, router[...])
        both = dot(low, wkv[...])
        turned = pltpu.roll(both, LANES // 2, 1)
        kv[span, :LANES] = jnp.where(half_lane, both, turned).astype(BF16)
        kv[span, LANES:] = jnp.where(half_lane, turned, both).astype(BF16)
    for tile in range(tiles):
        at = tile * TILE
        span = pl.ds(at, TILE)
        meta = jnp.concatenate(
            [
                sent[:, at : at + TILE],
                valid[:, at : at + TILE],
                expert[:, at : at + TILE],
                jnp.zeros((4, TILE), jnp.int32),
            ],
            axis=0,
        ).astype(F32)
        column = jnp.transpose(meta)
        own_sent, own_valid = column[:, 0:1], column[:, 1:2]
        first_id, second_id = column[:, 2:3], column[:, 3:4]
        glow[span, :] = jnp.where(own_valid > 0.5, cot[span, :].astype(F32), 0.0).astype(BF16)
        scored = logits[span, :]
        slot = lax.broadcasted_iota(jnp.int32, scored.shape, 1).astype(F32)
        pick0 = jnp.sum(jnp.where(slot == first_id, scored, 0.0), axis=-1, keepdims=True)
        pick1 = jnp.sum(jnp.where(slot == second_id, scored, 0.0), axis=-1, keepdims=True)
        most = jnp.maximum(pick0, pick1)
        raise0, raise1 = jnp.exp(pick0 - most), jnp.exp(pick1 - most)
        gate0 = raise0 / (raise0 + raise1)
        gate1 = raise1 / (raise0 + raise1)
        lane = lax.broadcasted_iota(jnp.int32, (TILE, 8), 1)
        gates[span, :] = jnp.where(
            lane == 0, gate0, jnp.where(lane == 1, gate1, jnp.where(lane == 2, first_id, second_id))
        )
        masks = pair_masks(first_id, second_id, pairs)
        q0 = jnp.zeros((TILE, LANES), F32)
        q1 = jnp.zeros((TILE, LANES), F32)
        for pair in range(pairs):
            block = queries[span, pair * LANES : (pair + 1) * LANES].astype(F32)
            q0 = jnp.where(masks[pair][0], block, q0)
            q1 = jnp.where(masks[pair][1], block, q1)
        picked = (jnp.concatenate([q0, q1], axis=0) * scale).astype(BF16)
        qsel[tile] = picked
        start, extent = window_of(tile, tiles)
        near = pl.ds(start, extent)
        scores = dot_nt(picked, kv[near, :LANES])
        same = own_sent == sent[:, start : start + extent].astype(F32)
        same = jnp.concatenate([same, same], axis=0)
        scores = jnp.where(same, scores, -1e30)
        weights = jnp.exp(scores - jnp.max(scores, axis=-1, keepdims=True))
        share = (weights * (1.0 / jnp.sum(weights, axis=-1, keepdims=True))).astype(BF16)
        chance[tile] = share
        context = dot(share, kv[near, LANES:])
        part0 = context[:TILE] * gate0
        part1 = context[TILE:] * gate1
        for pair in range(pairs):
            mixed[span, pair * LANES : (pair + 1) * LANES] = jnp.where(
                masks[pair][0], part0, jnp.where(masks[pair][1], part1, 0.0)
            ).astype(BF16)
    for at in range(0, rows, BIG):
        span = pl.ds(at, BIG)
        total = tok[span, :].astype(F32) + dot(mixed[span, :], wo[...])
        res[span, :] = total.astype(BF16)
        hat, _ = normed(total)
        low2[span, :] = (hat * as_row(gain2) + as_row(shift2)).astype(BF16)


def ffn_kernel(*refs, units, more):
    low2, glow, weights = refs[:3]
    at = 3
    if "rows" in more:
        out_in, second_in = refs[at : at + 2]
        at += 2
    if "weights" in more:
        contract_in, expand_in, bias_in = refs[at : at + 3]
        at += 3
    if "final" in more:
        out, second, contract_out, folded_out, bias_out, hidden, grad = refs[at:]
    else:
        out, second, contract_out, expand_out, bias_out, hidden, grad = refs[at:]
    rows = low2.shape[0]
    contract = weights.at[:units, :]
    expand = weights.at[units + 16 :, :units]
    bias = weights[units : units + 1, :units].astype(F32)
    bias_sum = bias_in[...] if "weights" in more else jnp.zeros((1, units), F32)
    for first in range(0, rows, BIG):
        span = pl.ds(first, BIG)
        preact = dot(low2[span, :], expand[...]) + bias
        cumulative = 0.5 * (1.0 + lax.erf(preact * (1.0 / math.sqrt(2.0))))
        bell = jnp.exp(-0.5 * preact * preact) * (1.0 / math.sqrt(2.0 * math.pi))
        high = (preact * cumulative).astype(BF16)
        hidden[span, :] = high
        slope = cumulative + preact * bell
        low_grad = (dot_nt(glow[span, :], contract[...]) * slope).astype(BF16)
        grad[span, :] = low_grad
        bias_sum += row_sum(low_grad.astype(F32))
        out_part = dot(high, contract[...])
        second_part = dot_nt(low_grad, expand[...])
        if "rows" in more:
            out_part += out_in[span, :].astype(F32)
            second_part += second_in[span, :].astype(F32)
        out[span, :] = out_part.astype(out.dtype)
        second[span, :] = second_part.astype(second.dtype)
    contract_sum = dot_tn(hidden[...], glow[...])
    expand_sum = dot_tn(low2[...], grad[...])
    if "weights" in more:
        contract_sum += contract_in[...].astype(F32)
        expand_sum += expand_in[...].astype(F32)
    bias_out[...] = bias_sum
    if "final" in more:
        contract_out[...] = contract_sum.astype(contract_out.dtype)
        for at in range(0, expand_sum.shape[0], units):
            block = expand_sum[at : at + units, :]
            folded_out[:, at : at + units] = block.astype(folded_out.dtype)
    else:
        contract_out[...] = contract_sum.astype(contract_out.dtype)
        expand_out[...] = expand_sum.astype(expand_out.dtype)


def ffn(rows_far, low2, glow, weights, weights_far, units, rows_in=None, weights_in=None,
        rows_out=("far", "far"), final=False, carry="far"):
    rows, width = low2.shape
    more = []
    operands = [low2, glow, weights]
    spaces = [rows_far, rows_far, weights_far]
    if final:
        more.append("final")
    if rows_in is not None:
        more.append("rows")
        operands += rows_in
        spaces += ["far" if rows_far == "near" else "near"] * 2
    if weights_in is not None:
        more.append("weights")
        operands += weights_in
        spaces += [carry, carry, "near"]
    scratch = [pltpu.VMEM((rows, units), BF16), pltpu.VMEM((rows, units), BF16)]
    if final:
        sums = [jax.ShapeDtypeStruct((units, width), BF16)] * 2
    else:
        sums = [
            jax.ShapeDtypeStruct((units, width), BF16), jax.ShapeDtypeStruct((width, units), BF16)
        ]
    sums_out = [carry] * len(sums)
    outs = placed_call(
        functools.partial(ffn_kernel, units=units, more=tuple(more)),
        "ffn",
        operands,
        spaces,
        [jax.ShapeDtypeStruct((rows, width), BF16)] * 2
        + sums
        + [jax.ShapeDtypeStruct((1, units), F32)],
        list(rows_out) + sums_out + ["near"],
        scratch,
    )
    return list(outs[:2]), list(outs[2:])


def back_kernel(
    place, second_own, second_got, unit_own, unit_peers,
    res, glow, wo, gates, mixed, kv, chance, qsel, tok, wq, wkv,
    gain1, shift1, gain2, router,
    tok_grad, keep, send,
    packed, low1, grad_res, grad_mixed, grad_q, grad_log, key_sum, value_sum, vectors,
):
    rows, width = tok.shape
    tiles = rows // TILE
    pairs = width // LANES
    scale = (wkv.shape[1] // 2) ** -0.5
    experts = router.shape[0]
    gain_one, gain_two = as_row(gain1), as_row(gain2)
    gain2_sum = shift2_sum = bias_sum = jnp.zeros((1, width), F32)
    for at in range(0, rows, BIG):
        span = pl.ds(at, BIG)
        hat, inverse = normed(res[span, :].astype(F32))
        second = second_own[span, :].astype(F32) + second_got[span, :].astype(F32)
        gain2_sum += row_sum(second * hat)
        shift2_sum += row_sum(second)
        outer = glow[span, :].astype(F32)
        bias_sum += row_sum(outer)
        grad = outer + norm_back(second, gain_two, hat, inverse)
        grad_res[span, :] = grad
        low_grad = grad.astype(BF16)
        low1[span, :] = low_grad
        grad_mixed[span, :] = dot_nt(low_grad, wo[...])
    packed[:, width : 2 * width] = dot_tn(mixed[...], low1[...]).astype(BF16)
    key_sum[...] = jnp.zeros_like(key_sum)
    value_sum[...] = jnp.zeros_like(value_sum)
    for tile in range(tiles):
        at = tile * TILE
        span = pl.ds(at, TILE)
        gate0, gate1 = gates[span, 0:1], gates[span, 1:2]
        first_id, second_id = gates[span, 2:3], gates[span, 3:4]
        masks = pair_masks(first_id, second_id, pairs)
        g0 = jnp.zeros((TILE, LANES), F32)
        g1 = jnp.zeros((TILE, LANES), F32)
        use0 = jnp.zeros((TILE, LANES), F32)
        use1 = jnp.zeros((TILE, LANES), F32)
        for pair in range(pairs):
            lanes = slice(pair * LANES, (pair + 1) * LANES)
            block = grad_mixed[span, lanes]
            both = block * mixed[span, lanes].astype(F32)
            g0 = jnp.where(masks[pair][0], block, g0)
            g1 = jnp.where(masks[pair][1], block, g1)
            use0 = jnp.where(masks[pair][0], both, use0)
            use1 = jnp.where(masks[pair][1], both, use1)
        use0 = jnp.sum(use0, axis=-1, keepdims=True)
        use1 = jnp.sum(use1, axis=-1, keepdims=True)
        turn = gate1 * use0 - gate0 * use1
        lane = lax.broadcasted_iota(jnp.int32, (TILE, LANES), 1).astype(F32)
        grad_log[span, :] = jnp.where(
            lane == first_id, turn, jnp.where(lane == second_id, -turn, 0.0)
        ).astype(BF16)
        grad_ctx = jnp.concatenate([g0 * gate0, g1 * gate1], axis=0).astype(BF16)
        delta = jnp.concatenate([use0, use1], axis=0)
        start, extent = window_of(tile, tiles)
        near = pl.ds(start, extent)
        grad_share = dot_nt(grad_ctx, kv[near, LANES:])
        share = chance[tile]
        raw = (share.astype(F32) * (grad_share - delta)).astype(BF16)
        grad_query = dot(raw, kv[near, :LANES]) * scale
        for pair in range(pairs):
            grad_q[span, pair * LANES : (pair + 1) * LANES] = jnp.where(
                masks[pair][0],
                grad_query[:TILE],
                jnp.where(masks[pair][1], grad_query[TILE:], 0.0),
            ).astype(BF16)
        key_sum[near, :] += dot_tn(raw, qsel[tile])
        value_sum[near, :] += dot_tn(share, grad_ctx)
    keys, values = key_sum[...], value_sum[...]
    keys = keys + pltpu.roll(keys, LANES // 2, 1)
    values = values + pltpu.roll(values, LANES // 2, 1)
    half_lane = lax.broadcasted_iota(jnp.int32, (rows, LANES), 1) < LANES // 2
    grad_kv = jnp.where(half_lane, keys, values).astype(BF16)
    gain1_sum = shift1_sum = jnp.zeros((1, width), F32)
    for at in range(0, rows, BIG):
        span = pl.ds(at, BIG)
        hat, inverse = normed(tok[span, :].astype(F32))
        low1[span, :] = (hat * gain_one + as_row(shift1)).astype(BF16)
        grad = (
            dot_nt(grad_q[span, :], wq[...])
            + dot_nt(grad_kv[at : at + BIG], wkv[...])
            + dot(grad_log[span, :experts], router[...])
        )
        gain1_sum += row_sum(grad * hat)
        shift1_sum += row_sum(grad)
        tok_grad[span, :] = (grad_res[span, :] + norm_back(grad, gain_one, hat, inverse)).astype(
            BF16
        )
    packed[:, :width] = dot_tn(low1[...], grad_q[...]).astype(BF16)
    packed[:, 2 * width : 2 * width + LANES] = dot_tn(low1[...], grad_kv).astype(BF16)
    vectors[...] = jnp.zeros_like(vectors)
    sums = (gain1_sum, shift1_sum, gain2_sum, shift2_sum, bias_sum)
    for at, values in enumerate(sums):
        vectors[VECTOR_ROW + at : VECTOR_ROW + at + 1, :] = values
    units = unit_own.shape[1]
    own = place[0]
    for step in range(unit_peers.shape[0] + 1):
        owner = own ^ (2 * step)
        part = unit_own[...] if step == 0 else unit_peers[step - 1 : step, :]
        vectors[pl.ds(VECTOR_ROW + len(sums) + owner, 1), :units] = part
    packed[:, 2 * width + LANES :] = (
        dot_tn(low1[...], grad_log[...]) + jnp.transpose(vectors[...])
    ).astype(BF16)
    half = width // 2
    mine = own % 2
    keep[...] = packed[pl.ds(pl.multiple_of(mine * half, half), half), :]
    send[...] = packed[pl.ds(pl.multiple_of((1 - mine) * half, half), half), :]


def unpack_kernel(
    place, mine, other,
    gain1, shift1, router, query, output, keyval, gain2, shift2, unit, bias,
    rest,
):
    half, width = mine.shape[0], query.shape[1]
    for end, values in ((place[0] % 2, mine), (1 - place[0] % 2, other)):
        span = pl.ds(pl.multiple_of(end * half, half), half)
        query[span, :] = values[:, :width].astype(F32)
        output[span, :] = values[:, width : 2 * width].astype(F32)
        keyval[span, :] = values[:, 2 * width : 2 * width + LANES].astype(F32)
        rest[span, :] = values[:, 2 * width + LANES :].astype(F32)
    rows = jnp.transpose(rest[...])
    router[...] = rows[: router.shape[0], :]
    for at, target in enumerate((gain1, shift1, gain2, shift2, bias)):
        target[...] = rows[VECTOR_ROW + at : VECTOR_ROW + at + 1, :]
    owner = lax.broadcasted_iota(jnp.int32, rows.shape, 0) - (VECTOR_ROW + 5)
    unit[...] = jnp.sum(jnp.where(owner == place[0], rows, 0.0), axis=0, keepdims=True)[
        :, : unit.shape[1]
    ]


def placed_call(kernel, name, operands, spaces, out_shape, out_spaces, scratch):
    where = {"far": pltpu.HBM, "near": pltpu.VMEM}
    lies = [pltpu.SMEM if space == "scalar" else pltpu.VMEM for space in spaces]
    operands = [
        pltpu.with_memory_space_constraint(item, where[space]) if space in where else item
        for item, space in zip(operands, spaces)
    ]
    results = [
        where[space](item.shape, item.dtype) if space in where else item
        for item, space in zip(out_shape, out_spaces)
    ]
    return pl.pallas_call(
        kernel,
        out_shape=results,
        in_specs=[pl.BlockSpec(memory_space=space) for space in lies],
        out_specs=[pl.BlockSpec(memory_space=pltpu.VMEM)] * len(results),
        scratch_shapes=scratch,
        compiler_params=pltpu.CompilerParams(vmem_limit_bytes=VMEM_LIMIT),
        cost_estimate=pl.CostEstimate(flops=1000, bytes_accessed=1000, transcendentals=0),
        name=name,
    )(*operands)


def swap(values, bit, devices):
    return lax.ppermute(values, AXES, [(at, at ^ bit) for at in range(devices)])


def halves(values, mine):
    size = values.shape[0] // 2
    keep = lax.dynamic_slice_in_dim(values, mine * size, size, 0)
    send = lax.dynamic_slice_in_dim(values, (1 - mine) * size, size, 0)
    return keep, send


def add_low(left, right):
    return (left.astype(F32) + right.astype(F32)).astype(BF16)


class Chain:
    def __init__(self, steps, place, devices):
        self.steps = list(steps)
        self.place, self.devices = place, devices
        self.values = self.keep = self.outgoing = None

    def mine(self, at):
        return (self.place // self.steps[at][1]) % 2

    def feed(self, values):
        self.values = values
        if self.steps and self.steps[0][0] == "cut":
            self.keep, self.outgoing = halves(values, self.mine(0))
        else:
            self.outgoing = values
        return self

    def feed_halves(self, keep, send):
        self.keep, self.outgoing = keep, send
        return self

    def send(self):
        return swap(self.outgoing, self.steps[0][1], self.devices)

    def take(self, got):
        kind = self.steps[0][0]
        if kind == "cut" and len(self.steps) > 1 and self.steps[1][0] == "cut":
            (keep, send), (keep_got, send_got) = (
                halves(item, self.mine(1)) for item in (self.keep, got)
            )
            self.outgoing = add_low(send, send_got)
            self.keep = add_low(keep, keep_got)
        else:
            if kind == "cut":
                values = add_low(self.keep, got)
            elif kind == "full":
                values = add_low(self.values, got)
            else:
                values = joined(self.values, got, self.mine(0))
            self.values = self.outgoing = values
        self.steps.pop(0)

    def run(self, steps):
        for _ in range(min(steps, len(self.steps))):
            self.take(self.send())
        return self.values


def plan(bits, whole=1):
    cut, full = bits[: len(bits) - whole], bits[len(bits) - whole :]
    return (
        [("cut", bit) for bit in cut]
        + [("full", bit) for bit in full]
        + [("join", bit) for bit in reversed(cut)]
    )


def sum_low(parts):
    return functools.reduce(jnp.add, [part.astype(F32) for part in parts]).astype(BF16)


def joined(values, got, mine):
    return jnp.where(
        mine == 0,
        jnp.concatenate([values, got], axis=0),
        jnp.concatenate([got, values], axis=0),
    )


def shards(
    n_dp,
    n_mp,
    tokens,
    sentence_ids,
    validity,
    expert_ids,
    cotangent,
    first_gain,
    first_shift,
    router,
    query_weight,
    output_weight,
    keyval_weight,
    second_gain,
    second_shift,
    expand_weight,
    expand_bias,
    contract_weight,
    contract_bias,
):
    devices = n_dp * n_mp
    rows, width = tokens.shape
    units = expand_weight.shape[1]
    tiles = rows // TILE
    _, extent = window_of(0, tiles)
    place = lax.axis_index(AXES)
    mp_place = lax.axis_index("mp")

    def row(vector):
        return vector.reshape(1, -1)

    def shape(*dims, dtype=BF16):
        return jax.ShapeDtypeStruct(dims, dtype)

    bias_rows = jnp.pad(expand_bias[None], ((0, 15), (0, width - units)))
    wide_expand = jnp.pad(expand_weight, ((0, 0), (0, width - units)))
    own = jnp.concatenate([contract_weight, bias_rows, wide_expand], axis=0)
    turned_router = router.T
    chips = n_mp // 2
    others = [swap(own, 2 * step, devices) for step in range(1, chips)]
    operands = [
        row(sentence_ids), row(validity), expert_ids.T, first_gain, first_shift, second_gain,
        second_shift, turned_router, tokens, query_weight, keyval_weight, cotangent, output_weight,
    ]
    res, low2, glow, mixed, qsel, kv, chance, gates = placed_call(
        attend_kernel,
        "attend",
        operands,
        ["far"] * len(operands),
        [shape(rows, width)] * 4
        + [
            shape(tiles, 2 * TILE, LANES),
            shape(rows, 2 * LANES),
            shape(tiles, 2 * TILE, extent),
            shape(rows, 8, dtype=F32),
        ],
        ["far", "near", "near"] + ["far"] * 5,
        [pltpu.VMEM((rows, width), BF16), pltpu.VMEM((rows, router.shape[1]), F32)],
    )
    low2_pair = swap(low2, 1, devices)
    glow_pair = swap(glow, 1, devices)
    dp_bits = [n_mp << at for at in range(n_dp.bit_length() - 1)]
    mp_bits = [1 << at for at in range(n_mp.bit_length() - 1)]
    rows_own, grads_own = ffn("near", low2, glow, own, "far", units)
    rows_pair, grads_own = ffn(
        None, low2_pair, glow_pair, own, "far", units, weights_in=grads_own, rows_out=(None, None),
        final=True,
    )
    contract_sum, expand_sum, unit_own = grads_own
    unit_peers = []
    waiting = []
    for step in range(1, chips):
        final = step == chips - 1
        rows_pair, grads = ffn(
            None,
            low2_pair,
            glow_pair,
            others[step - 1],
            None,
            units,
            rows_in=rows_pair,
            rows_out=(None, None),
        )
        if final:
            out_got, second_got = (swap(item, 1, devices) for item in rows_pair)
        rows_own, grads = ffn(
            "near",
            low2,
            glow,
            others[step - 1],
            None,
            units,
            rows_in=rows_own,
            weights_in=grads,
            rows_out=("far", "near" if final else "far"),
            final=True,
        )
        unit_peers.append(grads[2])
        waiting.append([swap(item, 2 * step, devices) for item in grads[:2]])
    scalars = jnp.full((1,), mp_place, jnp.int32)
    tok_grad, keep, send = placed_call(
        back_kernel,
        "back",
        [
            scalars, rows_own[1], second_got, unit_own, jnp.concatenate(unit_peers, axis=0),
            res, glow, output_weight, gates, mixed, kv, chance, qsel, tokens, query_weight,
            keyval_weight, first_gain, first_shift, second_gain, turned_router,
        ],
        ["scalar", "near", None, None, None, "far", "near"] + ["far"] * 13,
        [shape(rows, width)] + [shape(width // 2, 2 * width + 2 * LANES)] * 2,
        ["far", "near", "near"],
        [
            pltpu.VMEM((width, 2 * width + 2 * LANES), BF16),
            pltpu.VMEM((rows, width), BF16),
            pltpu.VMEM((rows, width), F32),
            pltpu.VMEM((rows, width), F32),
            pltpu.VMEM((rows, width), BF16),
            pltpu.VMEM((rows, LANES), BF16),
            pltpu.VMEM((rows, LANES), F32),
            pltpu.VMEM((rows, LANES), F32),
            pltpu.VMEM((LANES, width), F32),
        ],
    )
    order = mp_bits[:1] + dp_bits[:1] + mp_bits[1:] + dp_bits[1:]
    contract_got = [item[0] for item in waiting]
    expand_got = [item[1] for item in waiting]
    send, contract_got = lax.optimization_barrier((send, contract_got))
    first = Chain(plan(dp_bits[1:2] + dp_bits[:1] + dp_bits[2:], 1), place, devices)
    first.feed(sum_low([contract_sum, *contract_got]))
    second = Chain(plan(dp_bits, 1), place, devices)
    chain = Chain(plan(order, 1)[:-1], place, devices).feed_halves(keep, send)
    for at in range(len(chain.steps)):
        got = chain.send()
        if at == 1:
            got, expand_got = lax.optimization_barrier((got, expand_got))
            second.feed(sum_low([expand_sum, *expand_got]))
        chain.take(got)
    packed = chain.values
    layer = (
        res.astype(F32) + rows_own[0].astype(F32) + out_got.astype(F32) + contract_bias.astype(F32)
    ).astype(BF16)
    contract_sum = first.run(len(first.steps))
    contract_grad = contract_sum.astype(F32)
    other = swap(packed, mp_bits[0], devices)
    square = shape(width, width, dtype=F32)
    line = shape(1, width, dtype=F32)
    unpacked = placed_call(
        unpack_kernel,
        "unpack",
        [scalars, packed, other],
        ["scalar", None, None],
        [
            line, line, shape(router.shape[1], width, dtype=F32), square, square,
            shape(width, LANES, dtype=F32), line, line, shape(1, units, dtype=F32), line,
        ],
        [None] * 10,
        [pltpu.VMEM((width, LANES), F32)],
    )
    second.run(len(second.steps) - 1)
    got, unpacked, layer = lax.optimization_barrier((second.send(), unpacked, layer))
    second.take(got)
    expand_sum = second.values
    expand_grad = jnp.concatenate(
        [expand_sum[:, at : at + units] for at in range(0, width, units)], axis=0
    ).astype(F32)
    (
        gain1_grad, shift1_grad, router_grad, query_grad, output_grad, keyval_grad, gain2_grad,
        shift2_grad, unit_grad, bias_grad,
    ) = unpacked
    return (
        layer,
        tok_grad,
        gain1_grad[0],
        shift1_grad[0],
        router_grad.T,
        query_grad,
        output_grad,
        keyval_grad,
        gain2_grad[0],
        shift2_grad[0],
        expand_grad,
        unit_grad[0],
        contract_grad,
        bias_grad[0],
    )


def solution(mesh):
    tokens_spec = P(AXES, None)
    placed = (
        tokens_spec,
        P(AXES),
        P(AXES),
        tokens_spec,
        tokens_spec,
        P(),
        P(),
        P(),
        P(),
        P(),
        P(),
        P(),
        P(),
        P(None, "mp"),
        P("mp"),
        P("mp", None),
        P(),
    )
    return jax.shard_map(
        functools.partial(shards, mesh.shape["dp"], mesh.shape["mp"]),
        mesh=mesh,
        in_specs=placed,
        out_specs=(
            tokens_spec,
            tokens_spec,
            P(),
            P(),
            P(),
            P(),
            P(),
            P(),
            P(),
            P(),
            P(None, "mp"),
            P("mp"),
            P("mp", None),
            P(),
        ),
        check_vma=False,
    )
```
